128 devices in a mesh: rep: 2 (over z_hi), row: 4 (over x), col: 16 (over z_lo, y, core).
Axes of the slice: x: 4, y: 4, z: 4 (z_hi: 2, z_lo: 2; z = z_hi * 2 + z_lo), core: 2. Of those that a mesh axis runs over, the one named last changes fastest.
Arguments:
- tokens: bfloat16 [2048, 5120], P(('rep', 'col'), 'row'), may hold values from -6 to 6
- grad_out: bfloat16 [2048, 5120], P(('rep', 'col'), 'row'), may hold values from -6 to 6
- gate_weight: bfloat16 [2, 5120, 13824], P('rep', 'row', 'col'), may hold values from -0.078125 to 0.078125
- up_weight: bfloat16 [2, 5120, 13824], P('rep', 'row', 'col'), may hold values from -0.078125 to 0.078125
- down_weight: bfloat16 [2, 13824, 5120], P('rep', 'col', 'row'), may hold values from -0.0546875 to 0.0546875
- gate_buffer: bfloat16 [2, 5120, 13824], P('rep', 'row', 'col'), may hold values from -0.08984375 to 0.08984375
- up_buffer: bfloat16 [2, 5120, 13824], P('rep', 'row', 'col'), may hold values from -0.08984375 to 0.08984375
- down_buffer: bfloat16 [2, 13824, 5120], P('rep', 'col', 'row'), may hold values from -0.08984375 to 0.08984375
Outputs:
- token_grad: bfloat16 [2048, 5120], P(('rep', 'col'), 'row')
- gate_new: bfloat16 [5120, 13824], P('row', 'col')
- up_new: bfloat16 [5120, 13824], P('row', 'col')
- down_new: bfloat16 [13824, 5120], P('col', 'row')
- gate_moment: bfloat16 [5120, 13824], P('row', 'col')
- up_moment: bfloat16 [5120, 13824], P('row', 'col')
- down_moment: bfloat16 [13824, 5120], P('col', 'row')
The draws below stay inside these ranges and needn't reach their ends.
All inputs are finite; a program needn't handle non-finite values.
Results may differ from the reference program's by a relative error of at most 0.0053.
Values may be sent and summed in bfloat16 or wider, within the bound.
A program may use at most 128 MiB of HBM per device.

```python
import jax
import jax.numpy as jnp

D = 5120
FF = 13824
TOK = 1024
TOKENS = 2048
N_REP = 2


def steps_of(key, shape, pieces, least, high):
    loudness, own = 1.0, jax.random.fold_in(key, 6)
    for dim, blocks in pieces:
        draws = jnp.exp(jax.random.uniform(jax.random.fold_in(own, dim), (blocks,), jnp.float32, least / len(pieces), high / len(pieces)))
        loudness = loudness * jnp.repeat(draws, shape[dim] // blocks).reshape([-1 if axis == dim else 1 for axis in range(len(shape))])
    return loudness


def scatter_about(stream_key, dims, deviation, bound, shards=(), held_as=jnp.bfloat16):
    level = steps_of(stream_key, dims, shards, -0.22, 0.18) if shards else 1.0
    entries = jax.random.normal(stream_key, dims, jnp.float32) * deviation * level
    return jnp.minimum(jnp.maximum(entries, -bound), bound).astype(held_as)


def setup_inputs(seed: int = 0) -> dict:
    key_of = jax.random.split(jax.random.key(seed), 9)
    return {
        "tokens": scatter_about(key_of[0], (TOKENS, D), 1.0, 6.0, ((0, 32), (1, 4))),
        "grad_out": scatter_about(key_of[1], (TOKENS, D), 1.0, 6.0, ((0, 32), (1, 4))),
        "gate_weight": scatter_about(key_of[2], (N_REP, D, FF), D ** -0.5, 0.078125, ((0, 2), (1, 4), (2, 16))),
        "up_weight": scatter_about(key_of[3], (N_REP, D, FF), D ** -0.5, 0.078125, ((0, 2), (1, 4), (2, 16))),
        "down_weight": scatter_about(key_of[4], (N_REP, FF, D), FF ** -0.5, 0.0546875, ((0, 2), (1, 16), (2, 4))),
        "gate_buffer": scatter_about(key_of[5], (N_REP, D, FF), 0.015, 0.08984375, ((0, 2), (1, 4), (2, 16))),
        "up_buffer": scatter_about(key_of[6], (N_REP, D, FF), 0.015, 0.08984375, ((0, 2), (1, 4), (2, 16))),
        "down_buffer": scatter_about(key_of[7], (N_REP, FF, D), 0.015, 0.08984375, ((0, 2), (1, 16), (2, 4))),
    }


def momentum_step(weight, buffer, grad):
    new_buffer = 0.9 * buffer.astype(jnp.float32) + 0.1 * grad
    new_weight = weight.astype(jnp.float32) - 0.5 * (0.3 * grad + 0.7 * new_buffer)
    return new_weight.astype(jnp.bfloat16), new_buffer.astype(jnp.bfloat16)


def reference(tokens, grad_out, gate_weight, up_weight, down_weight, gate_buffer, up_buffer, down_buffer):
    grads_list = []
    totals = [jnp.zeros(gate_weight.shape[1:], jnp.float32), jnp.zeros(up_weight.shape[1:], jnp.float32),
              jnp.zeros(down_weight.shape[1:], jnp.float32), jnp.zeros(gate_weight.shape[1:], jnp.float32),
              jnp.zeros(up_weight.shape[1:], jnp.float32), jnp.zeros(down_weight.shape[1:], jnp.float32)]
    for replica in range(N_REP):
        inputs = tokens[replica * TOK:(replica + 1) * TOK]
        cotangent = grad_out[replica * TOK:(replica + 1) * TOK]
        w_gate = gate_weight[replica]
        w_up = up_weight[replica]
        w_down = down_weight[replica]
        gate = jnp.dot(inputs, w_gate, preferred_element_type=jnp.float32)
        up = jnp.dot(inputs, w_up, preferred_element_type=jnp.float32)
        back = jnp.dot(cotangent, w_down.T, preferred_element_type=jnp.float32)
        sig = jax.nn.sigmoid(gate)
        active = gate * sig
        hidden = (active * up).astype(jnp.bfloat16)
        d_gate = (back * up * sig * (1.0 + gate * (1.0 - sig))).astype(jnp.bfloat16)
        d_up = (back * active).astype(jnp.bfloat16)
        token_part = jnp.dot(d_gate, w_gate.T, preferred_element_type=jnp.float32)
        token_part = token_part + jnp.dot(d_up, w_up.T, preferred_element_type=jnp.float32)
        grads_list.append(token_part.astype(jnp.bfloat16))
        grad_gate = jnp.dot(inputs.T, d_gate, preferred_element_type=jnp.float32) / TOK
        grad_up = jnp.dot(inputs.T, d_up, preferred_element_type=jnp.float32) / TOK
        grad_down = jnp.dot(hidden.T, cotangent, preferred_element_type=jnp.float32) / TOK
        gate_w, gate_b = momentum_step(w_gate, gate_buffer[replica], grad_gate)
        up_w, up_b = momentum_step(w_up, up_buffer[replica], grad_up)
        down_w, down_b = momentum_step(w_down, down_buffer[replica], grad_down)
        updated = [gate_w, up_w, down_w, gate_b, up_b, down_b]
        totals = [total + item.astype(jnp.float32) for total, item in zip(totals, updated)]
    means = [(total / N_REP).astype(jnp.bfloat16) for total in totals]
    token_grad = jnp.concatenate(grads_list, axis=0)
    return (token_grad, means[0], means[1], means[2], means[3], means[4], means[5])
```

```python
import functools

import jax
import jax.numpy as jnp
from jax import lax
from jax.experimental import pallas as pl
from jax.experimental.pallas import tpu as pltpu
from jax.sharding import PartitionSpec as P

MESH = pl.DeviceIdType.MESH
F32, BF16 = jnp.float32, jnp.bfloat16

TOK = 1024
D = 1280
F = 864
BLK = 64
CH = 256
NP = D // CH
STEP = 16
STEP_D = 48
MIX = 1.85
LEAD = 1.35


def rows_of(i, n):
    return pl.ds(pl.multiple_of(i * n, n), n)


def contract(a, b, dim_a, dim_b):
    return lax.dot_general(
        a, b, (((dim_a,), (dim_b,)), ((), ())), preferred_element_type=F32
    )


def rebuild(lam):
    keep = 1.0 - lam
    return keep, lam - MIX * keep, lam / MIX, keep - lam / MIX


def kernel(
    x_in, g_in, wg_in, wu_in, wd_in, bg_in, bu_in, bd_in,
    tg_out, gw_out, uw_out, dw_out, gb_out, ub_out, db_out, qr_gu, qr_d, pr_gu, pr_d,
    xs, gs, wg, wu, wd, q_gu, q_d, stg, own_b, rcv, hid, dgt, dup,
    tp, tc, ty, tzs, tz, tgo, gt, gt_d, cin, cin_d, out, out_d, lam_l, lam_r,
    ld_s, b_s, tok_s, tok_r, q_s, q_r, p_s, p_r, lam_s, rs_s, rs_r, ag_s, ag_r,
    tc_s, ty_s, ty_r, tz_s, cin_s, out_s, tg_s,
):
    r, x, c = lax.axis_index("rep"), lax.axis_index("row"), lax.axis_index("col")
    k = lax.rem(c, 2)
    y = lax.rem(c // 2, 4)
    zl = c // 8

    def col_of(zl_, y_, k_):
        return zl_ * 8 + y_ * 2 + k_

    peer = (1 - r, x, c)
    sib = (r, x, col_of(zl, y, 1 - k))
    zn = (r, x, col_of(1 - zl, y, k))
    ydev = {d: (r, x, col_of(zl, lax.rem(y + d, 4), k)) for d in (1, 2, 3)}

    def xdev(d):
        return (r, lax.rem(x + d, 4), c)

    def load(src, dst, i):
        return pltpu.make_async_copy(src, dst, ld_s.at[i])

    own_rows = rows_of(c, BLK)
    loads = [
        load(x_in, xs.at[own_rows], 0),
        load(g_in, gs.at[own_rows], 1),
        load(wd_in, wd, 2),
        load(wg_in, wg, 3),
        load(wu_in, wu, 4),
    ]
    for cp in loads:
        cp.start()

    def load_b(src, p, s):
        return pltpu.make_async_copy(src.at[rows_of(p, CH)], cin.at[s], b_s.at[s])

    def load_bd(p, s):
        return pltpu.make_async_copy(bd_in.at[:, rows_of(p, CH)], cin_d.at[s], b_s.at[s])

    for s in range(2):
        load_bd(s, s).start()

    bar = pltpu.get_barrier_semaphore()
    partners = [peer, sib, zn] + [ydev[d] for d in (1, 2, 3)] + [xdev(d) for d in (1, 2, 3)]
    for dev in partners:
        pl.semaphore_signal(bar, 1, device_id=dev, device_id_type=MESH)
    pl.semaphore_wait(bar, len(partners))

    def remote(src, dst, ss, rs, dev):
        return pltpu.make_async_remote_copy(
            src_ref=src, dst_ref=dst, send_sem=ss, recv_sem=rs, device_id=dev, device_id_type=MESH
        )

    mats = (xs, gs)

    def tok(m, owner, n, dev):
        blk = mats[m].at[rows_of(owner, BLK)]
        return remote(blk, blk, tok_s.at[m, n], tok_r.at[m, owner], dev)

    zn_owner = col_of(1 - zl, y, k)
    y_owner = {d: col_of(zl, lax.rem(y + 4 - d, 4), k) for d in (1, 2, 3)}
    zy_owner = {d: col_of(1 - zl, lax.rem(y + 4 - d, 4), k) for d in (1, 2, 3)}

    def tok_list(m):
        return (
            [(c, 1, zn), (c, 0, sib)]
            + [(c, 1 + d, ydev[d]) for d in (1, 2, 3)]
            + [(zn_owner, 5 + d, ydev[d]) for d in (1, 2, 3)]
            + [(zn_owner, 5, sib)]
            + [(y_owner[d], 8 + d, sib) for d in (1, 2, 3)]
            + [(zy_owner[d], 11 + d, sib) for d in (1, 2, 3)]
        )

    sends = [tok_list(0), tok_list(1)]

    def tok_start(m, lo, hi):
        for owner, n, dev in sends[m][lo:hi]:
            tok(m, owner, n, dev).start()

    def tok_wait(m, owner):
        tok(m, owner, 0, sib).wait_recv()

    for m in range(2):
        loads[m].wait()
        tok_start(m, 0, 5)

    def squares(w, b):
        u = w - 0.315 * b
        v = (0.9 * MIX) * b
        return u * u, v * v

    def fold(v, lanes):
        return jnp.sum(v.reshape(v.shape[0] // 8, 8, lanes), axis=0)

    def choose(t, su, sv):
        lam = (jnp.sum(sv, keepdims=True) > jnp.sum(su, keepdims=True)).astype(F32)
        lam_l[t] = jnp.broadcast_to(lam, (8, 128))

    def q_copy_d(p):
        return remote(q_d.at[p], qr_d.at[p], q_s.at[p], q_r.at[p], peer)

    def q_copy(t, p):
        i = t * NP + p
        return remote(q_gu.at[i - NP], qr_gu.at[i - NP], q_s.at[i], q_r.at[i], peer)

    loads[2].wait()

    def q_down(p, carry):
        s = lax.rem(p, 2)
        load_bd(p, s).wait()

        def inner(i, acc):
            rr = rows_of(i, STEP_D)
            w = wd[rr, rows_of(p, CH)].astype(F32)
            b = cin_d[s, rr].astype(F32)
            q_d[p, rr] = (w + LEAD * b).astype(BF16)
            uu, vv = squares(w, b)
            return acc[0] + fold(uu, CH), acc[1] + fold(vv, CH)

        carry = lax.fori_loop(0, F // STEP_D, inner, carry)
        q_copy_d(p).start()

        @pl.when(p + 2 < NP)
        def _():
            load_bd(p + 2, s).start()

        return carry

    zero_d = jnp.zeros((8, CH), F32)
    choose(0, *lax.fori_loop(0, NP, q_down, (zero_d, zero_d)))

    def q_matrix(t, w_ref, b_in):
        for s in range(2):
            load_b(b_in, s, s).start()
        loads[2 + t].wait()

        def piece(p, carry):
            s = lax.rem(p, 2)
            load_b(b_in, p, s).wait()

            def inner(i, acc):
                rr = rows_of(i, STEP)
                w = w_ref[pl.ds(pl.multiple_of(p * CH + i * STEP, STEP), STEP)].astype(F32)
                b = cin[s, rr].astype(F32)
                q_gu[p + (t - 1) * NP, rr] = (w + LEAD * b).astype(BF16)
                uu, vv = squares(w, b)
                return acc[0] + fold(uu, F), acc[1] + fold(vv, F)

            carry = lax.fori_loop(0, CH // STEP, inner, carry)
            q_copy(t, p).start()

            @pl.when(p + 2 < NP)
            def _():
                load_b(b_in, p + 2, s).start()

            return carry

        zero = jnp.zeros((8, F), F32)
        choose(t, *lax.fori_loop(0, NP, piece, (zero, zero)))

    q_matrix(1, wg, bg_in)
    q_matrix(2, wu, bu_in)
    lam_copy = remote(lam_l, lam_r, lam_s.at[0], lam_s.at[1], peer)
    lam_copy.start()

    def forward_near(m):
        tok_wait(m, zn_owner)
        tok_start(m, 5, 9)
        for i, d in enumerate((1, 2, 3)):
            tok_wait(m, y_owner[d])
            tok_start(m, 9 + i, 10 + i)

    def forward_far(m):
        for i, d in enumerate((1, 2, 3)):
            tok_wait(m, zy_owner[d])
            tok_start(m, 12 + i, 13 + i)

    def from_sibling(m):
        for i in range(8):
            tok_wait(m, 2 * i + 1 - k)

    forward_near(0)
    forward_near(1)
    forward_far(0)
    from_sibling(0)

    def rs_copy(t, src, d):
        return remote(src, rcv.at[t, d - 1], rs_s.at[t, d - 1], rs_r.at[t, d - 1], xdev(d))

    def partial_in(t, w_ref):
        def step(i, _):
            j = lax.rem(x + i + 1, 4)
            stg[t, i] = jnp.dot(xs[rows_of(j, CH)], w_ref[...], preferred_element_type=F32)

            @pl.when(i < 3)
            def _():
                rs_copy(t, stg.at[t, i], i + 1).start()

            return 0

        lax.fori_loop(0, 4, step, 0)

    partial_in(0, wg)
    partial_in(1, wu)
    forward_far(1)
    from_sibling(1)

    for t in range(2):
        for d in (1, 2, 3):
            rs_copy(t, stg.at[t, d - 1], d).wait()

    def ag_copy(t, d, start=True):
        ref = (hid, dgt, dup)[t]
        rr = rows_of(x, CH)
        return remote(ref.at[rr], ref.at[rr], ag_s.at[t, d - 1], ag_r.at[t, d - 1], xdev(d))

    def ag_wait(t):
        ref = (hid, dgt, dup)[t]
        for d in (1, 2, 3):
            rr = rows_of(lax.rem(x + 4 - d, 4), CH)
            remote(ref.at[rr], ref.at[rr], ag_s.at[t, d - 1], ag_r.at[t, d - 1], xdev(d)).wait_recv()

    def make_hidden(i, _):
        rr = rows_of(i, STEP)
        gate = ((stg[0, 3, rr] + rcv[0, 0, rr]) + rcv[0, 1, rr]) + rcv[0, 2, rr]
        up = ((stg[1, 3, rr] + rcv[1, 0, rr]) + rcv[1, 1, rr]) + rcv[1, 2, rr]
        sig = jax.nn.sigmoid(gate)
        stg[0, 3, rr] = gate
        stg[1, 3, rr] = up
        hid[pl.ds(pl.multiple_of(x * CH + i * STEP, STEP), STEP)] = (gate * sig * up).astype(BF16)
        return 0

    lax.fori_loop(0, CH // STEP, make_hidden, 0)
    for d in (1, 2, 3):
        ag_copy(0, d).start()

    def partial_back(i, _):
        j = lax.rem(x + i + 1, 4)
        stg[0, i] = contract(gs[rows_of(j, CH)], wd[...], 1, 1)
        rs_copy(2, stg.at[0, i], i + 1).start()
        return 0

    lax.fori_loop(0, 3, partial_back, 0)
    own_b[...] = contract(gs[rows_of(x, CH)], wd[...], 1, 1)

    def p_copy_d(p):
        return remote(wd.at[:, rows_of(p, CH)], pr_d.at[p], p_s.at[p], p_r.at[p], peer)

    def p_copy(t, p):
        w_ref = (wg, wu)[t - 1]
        i = t * NP + p
        return remote(w_ref.at[rows_of(p, CH)], pr_gu.at[i - NP], p_s.at[i], p_r.at[i], peer)

    def moment(w, b, g, lam):
        g = g * (1.0 / TOK)
        new_b = 0.9 * b + 0.1 * g
        new_w = w - 0.5 * (0.3 * g + 0.7 * new_b)
        return jnp.where(lam > 0.5, new_w, new_b).astype(BF16)

    def step_down():
        for s in range(2):
            load_bd(s, s).start()
        lam = lam_l[0, 0:1, 0:1]

        def piece(p, _):
            cols = rows_of(p, CH)
            s = lax.rem(p, 2)
            gt_d[...] = contract(hid[...], gs[:, cols], 0, 0)
            load_bd(p, s).wait()

            def inner(i, _):
                rr = rows_of(i, STEP_D)
                w, b = wd[rr, cols].astype(F32), cin_d[s, rr].astype(F32)
                wd[rr, cols] = moment(w, b, gt_d[rr], lam)
                return 0

            lax.fori_loop(0, F // STEP_D, inner, 0)
            p_copy_d(p).start()

            @pl.when(p + 2 < NP)
            def _():
                load_bd(p + 2, s).start()

            return 0

        lax.fori_loop(0, NP, piece, 0)

    def step_matrix(t, w_ref, b_in, grads):
        for s in range(2):
            load_b(b_in, s, s).start()
        lam = lam_l[t, 0:1, 0:1]

        def piece(p, _):
            s = lax.rem(p, 2)
            gt[...] = contract(xs[:, rows_of(p, CH)], grads[...], 0, 0)
            load_b(b_in, p, s).wait()

            def inner(i, _):
                rr = rows_of(i, STEP)
                wr = pl.ds(pl.multiple_of(p * CH + i * STEP, STEP), STEP)
                w, b = w_ref[wr].astype(F32), cin[s, rr].astype(F32)
                w_ref[wr] = moment(w, b, gt[rr], lam)
                return 0

            lax.fori_loop(0, CH // STEP, inner, 0)
            p_copy(t, p).start()

            @pl.when(p + 2 < NP)
            def _():
                load_b(b_in, p + 2, s).start()

            return 0

        lax.fori_loop(0, NP, piece, 0)

    ag_wait(0)
    step_down()

    for d in (1, 2, 3):
        rs_copy(2, stg.at[0, d - 1], d).wait()

    def make_grads(i, _):
        rr = rows_of(i, STEP)
        back = ((own_b[rr] + rcv[2, 0, rr]) + rcv[2, 1, rr]) + rcv[2, 2, rr]
        gate, up = stg[0, 3, rr], stg[1, 3, rr]
        sig = jax.nn.sigmoid(gate)
        wr = pl.ds(pl.multiple_of(x * CH + i * STEP, STEP), STEP)
        dgt[wr] = (back * up * sig * (1.0 + gate * (1.0 - sig))).astype(BF16)
        dup[wr] = (back * (gate * sig)).astype(BF16)
        return 0

    lax.fori_loop(0, CH // STEP, make_grads, 0)
    for t in (1, 2):
        for d in (1, 2, 3):
            ag_copy(t, d).start()

    def token_part(grads, w_ref, first):
        def step(j, _):
            part = contract(grads[rows_of(j, CH)], w_ref[...], 1, 1).reshape(2, 2, BLK, D)
            two = rows_of(j, 2)
            if first:
                tp[two] = part
            else:
                tp[two] = tp[two] + part
            return 0

        lax.fori_loop(0, 4, step, 0)

    ag_wait(1)
    token_part(dgt, wg, True)
    step_matrix(1, wg, bg_in, dgt)
    ag_wait(2)
    token_part(dup, wu, False)
    tc_copy = remote(tp.at[:, 1 - k], tc, tc_s.at[0], tc_s.at[1], sib)
    tc_copy.start()
    step_matrix(2, wu, bu_in, dup)

    lam_copy.wait()

    def means(t, q_a, p_a, q_b, p_b):
        la = rebuild(lam_l[t, 0:1, 0:1])
        lb = rebuild(lam_r[t, 0:1, 0:1])
        q_a, p_a, q_b, p_b = (v.astype(F32) for v in (q_a, p_a, q_b, p_b))
        w = (la[0] * q_a + la[1] * p_a) + (lb[0] * q_b + lb[1] * p_b)
        b = (la[2] * q_a + la[3] * p_a) + (lb[2] * q_b + lb[3] * p_b)
        return (0.5 * w).astype(BF16), (0.5 * b).astype(BF16)

    def out_copy_d(p, s):
        cols = rows_of(p, CH)
        return (
            pltpu.make_async_copy(out_d.at[s, 0], dw_out.at[:, cols], out_s.at[s, 0]),
            pltpu.make_async_copy(out_d.at[s, 1], db_out.at[:, cols], out_s.at[s, 1]),
        )

    def combine_down():
        def piece(p, _):
            s = lax.rem(p, 2)
            q_copy_d(p).wait()
            p_copy_d(p).wait()
            ins = (
                pltpu.make_async_copy(qr_d.at[p], cin_d.at[0], cin_s.at[0]),
                pltpu.make_async_copy(pr_d.at[p], cin_d.at[1], cin_s.at[1]),
            )
            for cp in ins:
                cp.start()

            @pl.when(p >= 2)
            def _():
                for cp in out_copy_d(p - 2, s):
                    cp.wait()

            for cp in ins:
                cp.wait()

            def inner(i, _):
                rr = rows_of(i, STEP_D)
                w, b = means(0, q_d[p, rr], wd[rr, rows_of(p, CH)], cin_d[0, rr], cin_d[1, rr])
                out_d[s, 0, rr] = w
                out_d[s, 1, rr] = b
                return 0

            lax.fori_loop(0, F // STEP_D, inner, 0)
            for cp in out_copy_d(p, s):
                cp.start()
            return 0

        lax.fori_loop(0, NP, piece, 0)
        for p in (NP - 2, NP - 1):
            for cp in out_copy_d(p, p % 2):
                cp.wait()

    def combine(t, w_ref, w_out, b_out):
        def out_copy(p, s):
            rr = rows_of(p, CH)
            return (
                pltpu.make_async_copy(out.at[s, 0], w_out.at[rr], out_s.at[s, 0]),
                pltpu.make_async_copy(out.at[s, 1], b_out.at[rr], out_s.at[s, 1]),
            )

        def piece(p, _):
            s = lax.rem(p, 2)
            i = p + (t - 1) * NP
            q_copy(t, p).wait()
            p_copy(t, p).wait()
            ins = (
                pltpu.make_async_copy(qr_gu.at[i], cin.at[0], cin_s.at[0]),
                pltpu.make_async_copy(pr_gu.at[i], cin.at[1], cin_s.at[1]),
            )
            for cp in ins:
                cp.start()

            @pl.when(p >= 2)
            def _():
                for cp in out_copy(p - 2, s):
                    cp.wait()

            for cp in ins:
                cp.wait()

            def inner(n, _):
                rr = rows_of(n, STEP)
                wr = pl.ds(pl.multiple_of(p * CH + n * STEP, STEP), STEP)
                w, b = means(t, q_gu[i, rr], w_ref[wr], cin[0, rr], cin[1, rr])
                out[s, 0, rr] = w
                out[s, 1, rr] = b
                return 0

            lax.fori_loop(0, CH // STEP, inner, 0)
            for cp in out_copy(p, s):
                cp.start()
            return 0

        lax.fori_loop(0, NP, piece, 0)
        for p in (NP - 2, NP - 1):
            for cp in out_copy(p, p % 2):
                cp.wait()

    tc_copy.wait()

    def add_core(i, _):
        tc[i] = tc[i] + tp[i, k]
        return 0

    lax.fori_loop(0, 8, add_core, 0)

    def ty_copy(d, half):
        to = half * 4 + lax.rem(y + d, 4)
        return remote(tc.at[to], ty.at[d - 1, half], ty_s.at[d - 1, half], ty_r.at[d - 1, half], ydev[d])

    for d in (1, 2, 3):
        for half in range(2):
            ty_copy(d, half).start()

    combine_down()

    for d in (1, 2, 3):
        for half in range(2):
            ty_copy(d, half).wait()

    def along_y(half):
        return ((tc[half * 4 + y] + ty[0, half]) + ty[1, half]) + ty[2, half]

    tzs[...] = along_y(1 - zl).astype(BF16)
    tz_copy = remote(tzs, tz, tz_s.at[0], tz_s.at[1], zn)
    tz_copy.start()

    combine(1, wg, gw_out, gb_out)

    tz_copy.wait()
    tgo[...] = (along_y(zl) + tz[...].astype(F32)).astype(BF16)
    tg_copy = pltpu.make_async_copy(tgo, tg_out, tg_s.at[0])
    tg_copy.start()

    combine(2, wu, uw_out, ub_out)

    tg_copy.wait()
    for m in range(2):
        for owner, n, dev in sends[m]:
            tok(m, owner, n, dev).wait_send()
    for t in range(3):
        for d in (1, 2, 3):
            ag_copy(t, d).wait_send()


def body(tokens, grad_out, wg, wu, wd, bg, bu, bd):
    dma = pltpu.SemaphoreType.DMA
    whole = [(BLK, D)] + [(D, F), (D, F), (F, D)] * 2
    slots = [(2 * NP, CH, F), (NP, F, CH)] * 2
    scratch = [
        pltpu.VMEM((TOK, D), BF16),
        pltpu.VMEM((TOK, D), BF16),
        pltpu.VMEM((D, F), BF16),
        pltpu.VMEM((D, F), BF16),
        pltpu.VMEM((F, D), BF16),
        pltpu.VMEM((2 * NP, CH, F), BF16),
        pltpu.VMEM((NP, F, CH), BF16),
        pltpu.VMEM((2, 4, CH, F), F32),
        pltpu.VMEM((CH, F), F32),
        pltpu.VMEM((3, 3, CH, F), F32),
        pltpu.VMEM((TOK, F), BF16),
        pltpu.VMEM((TOK, F), BF16),
        pltpu.VMEM((TOK, F), BF16),
        pltpu.VMEM((8, 2, BLK, D), F32),
        pltpu.VMEM((8, BLK, D), F32),
        pltpu.VMEM((3, 2, BLK, D), F32),
        pltpu.VMEM((BLK, D), BF16),
        pltpu.VMEM((BLK, D), BF16),
        pltpu.VMEM((BLK, D), BF16),
        pltpu.VMEM((CH, F), F32),
        pltpu.VMEM((F, CH), F32),
        pltpu.VMEM((2, CH, F), BF16),
        pltpu.VMEM((2, F, CH), BF16),
        pltpu.VMEM((2, 2, CH, F), BF16),
        pltpu.VMEM((2, 2, F, CH), BF16),
        pltpu.VMEM((3, 8, 128), F32),
        pltpu.VMEM((3, 8, 128), F32),
        dma((5,)),
        dma((2,)),
        dma((2, 15)),
        dma((2, 16)),
        dma((3 * NP,)),
        dma((3 * NP,)),
        dma((3 * NP,)),
        dma((3 * NP,)),
        dma((2,)),
        dma((3, 3)),
        dma((3, 3)),
        dma((3, 3)),
        dma((3, 3)),
        dma((2,)),
        dma((3, 2)),
        dma((3, 2)),
        dma((2,)),
        dma((2,)),
        dma((2, 2)),
        dma((1,)),
    ]
    res = pl.pallas_call(
        kernel,
        out_shape=[jax.ShapeDtypeStruct(s, BF16) for s in whole + slots],
        in_specs=[pl.BlockSpec(memory_space=pl.ANY)] * 8,
        out_specs=[pl.BlockSpec(memory_space=pl.ANY)] * 11,
        scratch_shapes=scratch,
        compiler_params=pltpu.CompilerParams(
            collective_id=0, has_side_effects=True, vmem_limit_bytes=63 * 2**20
        ),
        cost_estimate=pl.CostEstimate(
            flops=16 * TOK * D * F, bytes_accessed=40 * D * F, transcendentals=2 * CH * F
        ),
    )(tokens, grad_out, wg[0], wu[0], wd[0], bg[0], bu[0], bd[0])
    return tuple(res[:7])


def solution(mesh):
    weights = (P("rep", "row", "col"), P("rep", "row", "col"), P("rep", "col", "row"))
    means = (P("row", "col"), P("row", "col"), P("col", "row"))
    return jax.shard_map(
        body,
        mesh=mesh,
        in_specs=(P(("rep", "col"), "row"),) * 2 + weights * 2,
        out_specs=(P(("rep", "col"), "row"),) + means * 2,
        check_vma=False,
    )
```

```python
import functools

import jax
import jax.numpy as jnp
from jax import lax
from jax.experimental import pallas as pl
from jax.experimental.pallas import tpu as pltpu
from jax.sharding import PartitionSpec as P

MESH = pl.DeviceIdType.MESH
F32, BF16 = jnp.float32, jnp.bfloat16

TOK = 1024
D = 1280
F = 864
BLK = 64
CH = 256
NP = D // CH
STEP = 16
STEP_D = 48
MIX = 1.85
LEAD = 1.35


def rows_of(i, n):
    return pl.ds(pl.multiple_of(i * n, n), n)


def contract(a, b, dim_a, dim_b):
    return lax.dot_general(
        a, b, (((dim_a,), (dim_b,)), ((), ())), preferred_element_type=F32
    )


def rebuild(lam):
    keep = 1.0 - lam
    return keep, lam - MIX * keep, lam / MIX, keep - lam / MIX


def kernel(
    x_in, g_in, wg_in, wu_in, wd_in, bg_in, bu_in, bd_in,
    tgo, wg, wu, wd, qg, qu, qd, qr,
    xs, gs, pr, stg, own_b, rcv, hid, dgt, dup,
    tp, tc, ty, tzs, tz, gt, cin, lam_l, lam_r,
    ld_s, b_s, tok_s, tok_r, q_s, q_r, p_s, p_r, lam_s, rs_s, rs_r, ag_s, ag_r,
    tc_s, ty_s, ty_r, tz_s, cin_s,
):
    r, x, c = lax.axis_index("rep"), lax.axis_index("row"), lax.axis_index("col")
    k = lax.rem(c, 2)
    y = lax.rem(c // 2, 4)
    zl = c // 8

    ws, qs = (wd, wg, wu), (qd, qg, qu)

    def col_of(zl_, y_, k_):
        return zl_ * 8 + y_ * 2 + k_

    peer = (1 - r, x, c)
    sib = (r, x, col_of(zl, y, 1 - k))
    zn = (r, x, col_of(1 - zl, y, k))
    ydev = {d: (r, x, col_of(zl, lax.rem(y + d, 4), k)) for d in (1, 2, 3)}

    def xdev(d):
        return (r, lax.rem(x + d, 4), c)

    bar = pltpu.get_barrier_semaphore()
    partners = [peer, sib, zn] + [ydev[d] for d in (1, 2, 3)] + [xdev(d) for d in (1, 2, 3)]
    for dev in partners:
        pl.semaphore_signal(bar, 1, device_id=dev, device_id_type=MESH)

    def load(src, dst, i):
        return pltpu.make_async_copy(src, dst, ld_s.at[i])

    own_rows = rows_of(c, BLK)
    loads = [
        load(x_in, xs.at[own_rows], 0),
        load(g_in, gs.at[own_rows], 1),
        load(wd_in, wd, 2),
        load(wg_in, wg, 3),
        load(wu_in, wu, 4),
    ]
    for cp in loads:
        cp.start()

    bs = (bd_in, bg_in, bu_in)

    def load_b(t, p, s):
        return pltpu.make_async_copy(bs[t].at[:, rows_of(p, CH)], cin.at[s], b_s.at[s])

    for s in range(2):
        load_b(0, s, s).start()

    def remote(src, dst, ss, rs, dev):
        return pltpu.make_async_remote_copy(
            src_ref=src, dst_ref=dst, send_sem=ss, recv_sem=rs, device_id=dev, device_id_type=MESH
        )

    mats = (xs, gs)

    def tok(m, owner, n, dev):
        blk = mats[m].at[rows_of(owner, BLK)]
        return remote(blk, blk, tok_s.at[m, n], tok_r.at[m, owner], dev)

    zn_owner = col_of(1 - zl, y, k)
    y_owner = {d: col_of(zl, lax.rem(y + 4 - d, 4), k) for d in (1, 2, 3)}
    zy_owner = {d: col_of(1 - zl, lax.rem(y + 4 - d, 4), k) for d in (1, 2, 3)}

    def tok_list(m):
        return (
            [(c, 1, zn), (c, 0, sib)]
            + [(c, 1 + d, ydev[d]) for d in (1, 2, 3)]
            + [(zn_owner, 5 + d, ydev[d]) for d in (1, 2, 3)]
            + [(zn_owner, 5, sib)]
            + [(y_owner[d], 8 + d, sib) for d in (1, 2, 3)]
            + [(zy_owner[d], 11 + d, sib) for d in (1, 2, 3)]
        )

    sends = [tok_list(0), tok_list(1)]

    def tok_start(m, lo, hi):
        for owner, n, dev in sends[m][lo:hi]:
            tok(m, owner, n, dev).start()

    def tok_wait(m, owner):
        tok(m, owner, 0, sib).wait_recv()

    def squares(w, b):
        u = w - 0.315 * b
        v = (0.9 * MIX) * b
        return u * u, v * v

    def fold(v):
        return jnp.sum(v.reshape(STEP_D // 8, 8, CH), axis=0)

    def q_copy(t, p):
        i = t * NP + p
        return remote(qs[t].at[:, rows_of(p, CH)], qr.at[i], q_s.at[i], q_r.at[i], peer)

    def q_piece(t, p, carry):
        s = lax.rem(p, 2)
        cols = rows_of(p, CH)
        load_b(t, p, s).wait()

        def inner(i, acc):
            rr = rows_of(i, STEP_D)
            w = ws[t][rr, cols].astype(F32)
            b = cin[s, rr].astype(F32)
            qs[t][rr, cols] = (w + LEAD * b).astype(BF16)
            uu, vv = squares(w, b)
            return acc[0] + fold(uu), acc[1] + fold(vv)

        return lax.fori_loop(0, F // STEP_D, inner, carry)

    def q_next(t, p):
        q_copy(t, p).start()

        @pl.when(p + 2 < NP)
        def _():
            load_b(t, p + 2, lax.rem(p, 2)).start()

    def choose(t, su, sv):
        lam = (jnp.sum(sv, keepdims=True) > jnp.sum(su, keepdims=True)).astype(F32)
        lam_l[t] = jnp.broadcast_to(lam, (8, 128))

    def q_rest(t, p, carry):
        carry = q_piece(t, p, carry)
        q_next(t, p)
        return carry

    zero = jnp.zeros((8, CH), F32)
    loads[2].wait()
    carry = q_piece(0, jnp.int32(0), (zero, zero))
    pl.semaphore_wait(bar, len(partners))
    for m in range(2):
        loads[m].wait()
        tok_start(m, 0, 5)
    q_next(0, jnp.int32(0))
    choose(0, *lax.fori_loop(1, NP, functools.partial(q_rest, 0), carry))
    for t in (1, 2):
        for s in range(2):
            load_b(t, s, s).start()
        loads[2 + t].wait()
        choose(t, *lax.fori_loop(0, NP, functools.partial(q_rest, t), (zero, zero)))
    lam_copy = remote(lam_l, lam_r, lam_s.at[0], lam_s.at[1], peer)
    lam_copy.start()

    def forward_near(m):
        tok_wait(m, zn_owner)
        tok_start(m, 5, 9)
        for i, d in enumerate((1, 2, 3)):
            tok_wait(m, y_owner[d])
            tok_start(m, 9 + i, 10 + i)

    def forward_far(m):
        for i, d in enumerate((1, 2, 3)):
            tok_wait(m, zy_owner[d])
            tok_start(m, 12 + i, 13 + i)

    def from_sibling(m):
        for i in range(8):
            tok_wait(m, 2 * i + 1 - k)

    forward_near(0)
    forward_near(1)
    forward_far(0)
    from_sibling(0)

    def rs_copy(t, src, d):
        return remote(src, rcv.at[t, d - 1], rs_s.at[t, d - 1], rs_r.at[t, d - 1], xdev(d))

    def partial_in(t, w_ref):
        def step(i, _):
            j = lax.rem(x + i + 1, 4)
            stg[t, i] = contract(xs[rows_of(j, CH)], w_ref[...], 1, 1)

            @pl.when(i < 3)
            def _():
                rs_copy(t, stg.at[t, i], i + 1).start()

            return 0

        lax.fori_loop(0, 4, step, 0)

    partial_in(0, wg)
    partial_in(1, wu)
    forward_far(1)
    from_sibling(1)

    for t in range(2):
        for d in (1, 2, 3):
            rs_copy(t, stg.at[t, d - 1], d).wait()

    def ag_copy(t, d, start=True):
        ref = (hid, dgt, dup)[t]
        rr = rows_of(x, CH)
        return remote(ref.at[rr], ref.at[rr], ag_s.at[t, d - 1], ag_r.at[t, d - 1], xdev(d))

    def ag_wait(t):
        ref = (hid, dgt, dup)[t]
        for d in (1, 2, 3):
            rr = rows_of(lax.rem(x + 4 - d, 4), CH)
            remote(ref.at[rr], ref.at[rr], ag_s.at[t, d - 1], ag_r.at[t, d - 1], xdev(d)).wait_recv()

    def make_hidden(i, _):
        rr = rows_of(i, STEP)
        gate = ((stg[0, 3, rr] + rcv[0, 0, rr]) + rcv[0, 1, rr]) + rcv[0, 2, rr]
        up = ((stg[1, 3, rr] + rcv[1, 0, rr]) + rcv[1, 1, rr]) + rcv[1, 2, rr]
        sig = jax.nn.sigmoid(gate)
        stg[0, 3, rr] = gate
        stg[1, 3, rr] = up
        hid[pl.ds(pl.multiple_of(x * CH + i * STEP, STEP), STEP)] = (gate * sig * up).astype(BF16)
        return 0

    lax.fori_loop(0, CH // STEP, make_hidden, 0)
    for d in (1, 2, 3):
        ag_copy(0, d).start()

    def partial_back(i, _):
        j = lax.rem(x + i + 1, 4)
        stg[0, i] = contract(gs[rows_of(j, CH)], wd[...], 1, 1)
        rs_copy(2, stg.at[0, i], i + 1).start()
        return 0

    lax.fori_loop(0, 3, partial_back, 0)
    own_b[...] = contract(gs[rows_of(x, CH)], wd[...], 1, 1)

    def p_copy(t, p):
        i = t * NP + p
        return remote(ws[t].at[:, rows_of(p, CH)], pr.at[i], p_s.at[i], p_r.at[i], peer)

    def step_matrix(t, left, right):
        for s in range(2):
            load_b(t, s, s).start()
        lam = lam_l[t, 0:1, 0:1]

        def piece(p, _):
            cols = rows_of(p, CH)
            s = lax.rem(p, 2)
            gt[...] = contract(left[...], right[:, cols], 0, 0)
            load_b(t, p, s).wait()

            def inner(i, _):
                rr = rows_of(i, STEP_D)
                w, b = ws[t][rr, cols].astype(F32), cin[s, rr].astype(F32)
                g = gt[rr] * (1.0 / TOK)
                new_b = 0.9 * b + 0.1 * g
                new_w = w - 0.5 * (0.3 * g + 0.7 * new_b)
                ws[t][rr, cols] = jnp.where(lam > 0.5, new_w, new_b).astype(BF16)
                return 0

            lax.fori_loop(0, F // STEP_D, inner, 0)
            p_copy(t, p).start()

            @pl.when(p + 2 < NP)
            def _():
                load_b(t, p + 2, s).start()

            return 0

        lax.fori_loop(0, NP, piece, 0)

    ag_wait(0)
    step_matrix(0, hid, gs)

    for d in (1, 2, 3):
        rs_copy(2, stg.at[0, d - 1], d).wait()

    def make_grads(i, _):
        rr = rows_of(i, STEP)
        back = ((own_b[rr] + rcv[2, 0, rr]) + rcv[2, 1, rr]) + rcv[2, 2, rr]
        gate, up = stg[0, 3, rr], stg[1, 3, rr]
        sig = jax.nn.sigmoid(gate)
        wr = pl.ds(pl.multiple_of(x * CH + i * STEP, STEP), STEP)
        dgt[wr] = (back * up * sig * (1.0 + gate * (1.0 - sig))).astype(BF16)
        dup[wr] = (back * (gate * sig)).astype(BF16)
        return 0

    lax.fori_loop(0, CH // STEP, make_grads, 0)
    for t in (1, 2):
        for d in (1, 2, 3):
            ag_copy(t, d).start()

    def token_part(grads, w_ref, first):
        def step(j, _):
            part = jnp.dot(grads[rows_of(j, CH)], w_ref[...], preferred_element_type=F32)
            part = part.reshape(2, 2, BLK, D)
            two = rows_of(j, 2)
            if first:
                tp[two] = part
            else:
                tp[two] = tp[two] + part
            return 0

        lax.fori_loop(0, 4, step, 0)

    ag_wait(1)
    token_part(dgt, wg, True)
    step_matrix(1, dgt, xs)
    ag_wait(2)
    token_part(dup, wu, False)
    tc_copy = remote(tp.at[:, 1 - k], tc, tc_s.at[0], tc_s.at[1], sib)
    tc_copy.start()
    step_matrix(2, dup, xs)

    lam_copy.wait()

    def means(t, q_a, p_a, q_b, p_b):
        la = rebuild(lam_l[t, 0:1, 0:1])
        lb = rebuild(lam_r[t, 0:1, 0:1])
        q_a, p_a, q_b, p_b = (v.astype(F32) for v in (q_a, p_a, q_b, p_b))
        w = (la[0] * q_a + la[1] * p_a) + (lb[0] * q_b + lb[1] * p_b)
        b = (la[2] * q_a + la[3] * p_a) + (lb[2] * q_b + lb[3] * p_b)
        return (0.5 * w).astype(BF16), (0.5 * b).astype(BF16)

    def load_q(t, p, s):
        return pltpu.make_async_copy(qr.at[t * NP + p], cin.at[s], cin_s.at[s])

    def combine(t):
        for s in range(2):
            q_copy(t, s).wait()
            load_q(t, s, s).start()

        def piece(p, _):
            s = lax.rem(p, 2)
            i = t * NP + p
            cols = rows_of(p, CH)
            load_q(t, p, s).wait()
            p_copy(t, p).wait()

            def inner(n, _):
                rr = rows_of(n, STEP_D)
                w, b = means(t, qs[t][rr, cols], ws[t][rr, cols], cin[s, rr], pr[i, rr])
                ws[t][rr, cols] = w
                qs[t][rr, cols] = b
                return 0

            lax.fori_loop(0, F // STEP_D, inner, 0)

            @pl.when(p + 2 < NP)
            def _():
                q_copy(t, p + 2).wait()
                load_q(t, p + 2, s).start()

            return 0

        lax.fori_loop(0, NP, piece, 0)

    tc_copy.wait()

    def add_core(i, _):
        tc[i] = tc[i] + tp[i, k]
        return 0

    lax.fori_loop(0, 8, add_core, 0)

    def ty_copy(d, half):
        to = half * 4 + lax.rem(y + d, 4)
        return remote(tc.at[to], ty.at[d - 1, half], ty_s.at[d - 1, half], ty_r.at[d - 1, half], ydev[d])

    for d in (1, 2, 3):
        for half in range(2):
            ty_copy(d, half).start()

    combine(0)

    for d in (1, 2, 3):
        for half in range(2):
            ty_copy(d, half).wait()

    def along_y(half):
        return ((tc[half * 4 + y] + ty[0, half]) + ty[1, half]) + ty[2, half]

    tzs[...] = along_y(1 - zl).astype(BF16)
    tz_copy = remote(tzs, tz, tz_s.at[0], tz_s.at[1], zn)
    tz_copy.start()

    combine(1)

    tz_copy.wait()
    tgo[...] = (along_y(zl) + tz[...].astype(F32)).astype(BF16)

    combine(2)

    for m in range(2):
        for owner, n, dev in sends[m]:
            tok(m, owner, n, dev).wait_send()
    for t in range(3):
        for d in (1, 2, 3):
            ag_copy(t, d).wait_send()


def body(tokens, grad_out, wg, wu, wd, bg, bu, bd):
    dma = pltpu.SemaphoreType.DMA
    whole = [(BLK, D)] + [(F, D)] * 6
    scratch = [
        pltpu.VMEM((TOK, D), BF16),
        pltpu.VMEM((TOK, D), BF16),
        pltpu.VMEM((3 * NP, F, CH), BF16),
        pltpu.VMEM((2, 4, CH, F), F32),
        pltpu.VMEM((CH, F), F32),
        pltpu.VMEM((3, 3, CH, F), F32),
        pltpu.VMEM((TOK, F), BF16),
        pltpu.VMEM((TOK, F), BF16),
        pltpu.VMEM((TOK, F), BF16),
        pltpu.VMEM((8, 2, BLK, D), F32),
        pltpu.VMEM((8, BLK, D), F32),
        pltpu.VMEM((3, 2, BLK, D), F32),
        pltpu.VMEM((BLK, D), BF16),
        pltpu.VMEM((BLK, D), BF16),
        pltpu.VMEM((F, CH), F32),
        pltpu.VMEM((2, F, CH), BF16),
        pltpu.VMEM((3, 8, 128), F32),
        pltpu.VMEM((3, 8, 128), F32),
        dma((5,)),
        dma((2,)),
        dma((2, 15)),
        dma((2, 16)),
        dma((3 * NP,)),
        dma((3 * NP,)),
        dma((3 * NP,)),
        dma((3 * NP,)),
        dma((2,)),
        dma((3, 3)),
        dma((3, 3)),
        dma((3, 3)),
        dma((3, 3)),
        dma((2,)),
        dma((3, 2)),
        dma((3, 2)),
        dma((2,)),
        dma((2,)),
    ]
    res = pl.pallas_call(
        kernel,
        out_shape=[pltpu.VMEM(s, BF16) for s in whole] + [jax.ShapeDtypeStruct((3 * NP, F, CH), BF16)],
        in_specs=[pl.BlockSpec(memory_space=pl.ANY)] * 8,
        out_specs=[pl.BlockSpec(memory_space=pltpu.VMEM)] * 7 + [pl.BlockSpec(memory_space=pl.ANY)],
        scratch_shapes=scratch,
        compiler_params=pltpu.CompilerParams(
            collective_id=0, has_side_effects=True, vmem_limit_bytes=48 * 2**20
        ),
        cost_estimate=pl.CostEstimate(
            flops=16 * TOK * D * F, bytes_accessed=40 * D * F, transcendentals=2 * CH * F
        ),
    )(tokens, grad_out, wg[0].T, wu[0].T, wd[0], bg[0].T, bu[0].T, bd[0])
    tg, gw, uw, dw, gb, ub, db = res[:7]
    return tg, gw.T, uw.T, dw, gb.T, ub.T, db


def solution(mesh):
    weights = (P("rep", "row", "col"), P("rep", "row", "col"), P("rep", "col", "row"))
    means = (P("row", "col"), P("row", "col"), P("col", "row"))
    return jax.shard_map(
        body,
        mesh=mesh,
        in_specs=(P(("rep", "col"), "row"),) * 2 + weights * 2,
        out_specs=(P(("rep", "col"), "row"),) + means * 2,
        check_vma=False,
    )
```

```python
import functools

import jax
import jax.numpy as jnp
from jax import lax
from jax.experimental import pallas as pl
from jax.experimental.pallas import tpu as pltpu
from jax.sharding import PartitionSpec as P

MESH = pl.DeviceIdType.MESH
F32, BF16 = jnp.float32, jnp.bfloat16

TOK = 1024
D = 1280
F = 864
BLK = 64
CH = 256
NP = D // CH
PARTS = 3
PART = F // PARTS
STEP = 16
STEP_D = 48
MIX = 1.85
LEAD = 1.35


def rows_of(i, n):
    return pl.ds(pl.multiple_of(i * n, n), n)


def contract(a, b, dim_a, dim_b):
    return lax.dot_general(
        a, b, (((dim_a,), (dim_b,)), ((), ())), preferred_element_type=F32
    )


def rebuild(lam):
    keep = 1.0 - lam
    return keep, lam - MIX * keep, lam / MIX, keep - lam / MIX


def kernel(
    x_in, g_in, wg_in, wu_in, wd_in, bg_in, bu_in, bd_in,
    tgo, wg, wu, wd, qg, qu, qd, qr,
    xs, gs, pr, stg, own_b, rcv, hid, dgt, dup,
    tp, tc, ty, tzs, tz, gt, cin, lam_l, lam_r,
    ld_s, b_s, tok_s, tok_r, q_s, q_r, p_s, p_r, lam_s, rs_s, rs_r, ag_s, ag_r,
    tc_s, ty_s, ty_r, tz_s, cin_s,
):
    r, x, c = lax.axis_index("rep"), lax.axis_index("row"), lax.axis_index("col")
    k = lax.rem(c, 2)
    y = lax.rem(c // 2, 4)
    zl = c // 8

    ws, qs = (wd, wg, wu), (qd, qg, qu)

    def col_of(zl_, y_, k_):
        return zl_ * 8 + y_ * 2 + k_

    peer = (1 - r, x, c)
    sib = (r, x, col_of(zl, y, 1 - k))
    zn = (r, x, col_of(1 - zl, y, k))
    ydev = {d: (r, x, col_of(zl, lax.rem(y + d, 4), k)) for d in (1, 2, 3)}

    def xdev(d):
        return (r, lax.rem(x + d, 4), c)

    bar = pltpu.get_barrier_semaphore()
    partners = [peer, sib, zn] + [ydev[d] for d in (1, 2, 3)] + [xdev(d) for d in (1, 2, 3)]
    for dev in partners:
        pl.semaphore_signal(bar, 1, device_id=dev, device_id_type=MESH)

    def load(src, dst, i):
        return pltpu.make_async_copy(src, dst, ld_s.at[i])

    own_rows = rows_of(c, BLK)
    loads = [
        load(x_in, xs.at[own_rows], 0),
        load(g_in, gs.at[own_rows], 1),
        load(wd_in, wd, 2),
        load(wg_in, wg, 3),
        load(wu_in, wu, 4),
    ]
    for cp in loads:
        cp.start()

    bs = (bd_in, bg_in, bu_in)

    def load_b(t, p, s):
        return pltpu.make_async_copy(bs[t].at[:, rows_of(p, CH)], cin.at[s], b_s.at[s])

    for s in range(2):
        load_b(0, s, s).start()

    def remote(src, dst, ss, rs, dev):
        return pltpu.make_async_remote_copy(
            src_ref=src, dst_ref=dst, send_sem=ss, recv_sem=rs, device_id=dev, device_id_type=MESH
        )

    mats = (xs, gs)

    def tok(m, owner, n, dev):
        blk = mats[m].at[rows_of(owner, BLK)]
        return remote(blk, blk, tok_s.at[m, n], tok_r.at[m, owner], dev)

    zn_owner = col_of(1 - zl, y, k)
    y_owner = {d: col_of(zl, lax.rem(y + 4 - d, 4), k) for d in (1, 2, 3)}
    zy_owner = {d: col_of(1 - zl, lax.rem(y + 4 - d, 4), k) for d in (1, 2, 3)}

    def tok_list(m):
        return (
            [(c, 1, zn), (c, 0, sib)]
            + [(c, 1 + d, ydev[d]) for d in (1, 2, 3)]
            + [(zn_owner, 5 + d, ydev[d]) for d in (1, 2, 3)]
            + [(zn_owner, 5, sib)]
            + [(y_owner[d], 8 + d, sib) for d in (1, 2, 3)]
            + [(zy_owner[d], 11 + d, sib) for d in (1, 2, 3)]
        )

    sends = [tok_list(0), tok_list(1)]

    def tok_start(m, lo, hi):
        for owner, n, dev in sends[m][lo:hi]:
            tok(m, owner, n, dev).start()

    def tok_wait(m, owner):
        tok(m, owner, 0, sib).wait_recv()

    def squares(w, b):
        u = w - 0.315 * b
        v = (0.9 * MIX) * b
        return u * u, v * v

    def fold(v):
        return jnp.sum(v.reshape(STEP_D // 8, 8, CH), axis=0)

    def q_copy(t, p):
        i = t * NP + p
        return remote(qs[t].at[:, rows_of(p, CH)], qr.at[i], q_s.at[i], q_r.at[i], peer)

    def q_piece(t, p, carry):
        s = lax.rem(p, 2)
        cols = rows_of(p, CH)
        load_b(t, p, s).wait()

        def inner(i, acc):
            rr = rows_of(i, STEP_D)
            w = ws[t][rr, cols].astype(F32)
            b = cin[s, rr].astype(F32)
            qs[t][rr, cols] = (w + LEAD * b).astype(BF16)
            uu, vv = squares(w, b)
            return acc[0] + fold(uu), acc[1] + fold(vv)

        return lax.fori_loop(0, F // STEP_D, inner, carry)

    def q_next(t, p):
        q_copy(t, p).start()

        @pl.when(p + 2 < NP)
        def _():
            load_b(t, p + 2, lax.rem(p, 2)).start()

    def choose(t, su, sv):
        lam = (jnp.sum(sv, keepdims=True) > jnp.sum(su, keepdims=True)).astype(F32)
        lam_l[t] = jnp.broadcast_to(lam, (8, 128))

    def q_rest(t, p, carry):
        carry = q_piece(t, p, carry)
        q_next(t, p)
        return carry

    zero = jnp.zeros((8, CH), F32)
    loads[2].wait()
    carry = q_piece(0, jnp.int32(0), (zero, zero))
    pl.semaphore_wait(bar, len(partners))
    loads[0].wait()
    tok_start(0, 0, 5)
    loads[1].wait()
    tok_start(1, 0, 1)
    q_next(0, jnp.int32(0))
    choose(0, *lax.fori_loop(1, NP, functools.partial(q_rest, 0), carry))
    for t in (1, 2):
        for s in range(2):
            load_b(t, s, s).start()
        loads[2 + t].wait()
        choose(t, *lax.fori_loop(0, NP, functools.partial(q_rest, t), (zero, zero)))
    lam_copy = remote(lam_l, lam_r, lam_s.at[0], lam_s.at[1], peer)
    lam_copy.start()

    def forward_near(m):
        tok_wait(m, zn_owner)
        tok_start(m, 5, 9)
        for i, d in enumerate((1, 2, 3)):
            tok_wait(m, y_owner[d])
            tok_start(m, 9 + i, 10 + i)

    def forward_far(m):
        for i, d in enumerate((1, 2, 3)):
            tok_wait(m, zy_owner[d])
            tok_start(m, 12 + i, 13 + i)

    def from_sibling(m):
        for i in range(8):
            tok_wait(m, 2 * i + 1 - k)

    forward_near(0)
    tok_start(1, 1, 5)
    forward_far(0)
    from_sibling(0)

    def rs_copy(t, src, d):
        return remote(src, rcv.at[t, d - 1], rs_s.at[t, d - 1], rs_r.at[t, d - 1], xdev(d))

    def partial_in(t, w_ref):
        def step(i, _):
            j = lax.rem(x + i + 1, 4)
            stg[t, i] = contract(xs[rows_of(j, CH)], w_ref[...], 1, 1)

            @pl.when(i < 3)
            def _():
                rs_copy(t, stg.at[t, i], i + 1).start()

            return 0

        lax.fori_loop(0, 4, step, 0)

    partial_in(0, wg)
    forward_near(1)
    partial_in(1, wu)
    forward_far(1)
    from_sibling(1)

    for t in range(2):
        for d in (1, 2, 3):
            rs_copy(t, stg.at[t, d - 1], d).wait()

    def ag_copy(t, d, start=True):
        ref = (hid, dgt, dup)[t]
        rr = rows_of(x, CH)
        return remote(ref.at[rr], ref.at[rr], ag_s.at[t, d - 1], ag_r.at[t, d - 1], xdev(d))

    def ag_wait(t):
        ref = (hid, dgt, dup)[t]
        for d in (1, 2, 3):
            rr = rows_of(lax.rem(x + 4 - d, 4), CH)
            remote(ref.at[rr], ref.at[rr], ag_s.at[t, d - 1], ag_r.at[t, d - 1], xdev(d)).wait_recv()

    def make_hidden(i, _):
        rr = rows_of(i, STEP)
        gate = ((stg[0, 3, rr] + rcv[0, 0, rr]) + rcv[0, 1, rr]) + rcv[0, 2, rr]
        up = ((stg[1, 3, rr] + rcv[1, 0, rr]) + rcv[1, 1, rr]) + rcv[1, 2, rr]
        sig = jax.nn.sigmoid(gate)
        stg[0, 3, rr] = gate
        stg[1, 3, rr] = up
        hid[pl.ds(pl.multiple_of(x * CH + i * STEP, STEP), STEP)] = (gate * sig * up).astype(BF16)
        return 0

    lax.fori_loop(0, CH // STEP, make_hidden, 0)
    for d in (1, 2, 3):
        ag_copy(0, d).start()

    def partial_back(i, _):
        j = lax.rem(x + i + 1, 4)
        stg[0, i] = contract(gs[rows_of(j, CH)], wd[...], 1, 1)
        rs_copy(2, stg.at[0, i], i + 1).start()
        return 0

    lax.fori_loop(0, 3, partial_back, 0)
    own_b[...] = contract(gs[rows_of(x, CH)], wd[...], 1, 1)

    def p_copy(t, p, h):
        i = t * NP + p
        rr = rows_of(h, PART)
        return remote(ws[t].at[rr, rows_of(p, CH)], pr.at[i, rr], p_s.at[i, h], p_r.at[i, h], peer)

    def step_matrix(t, left, right):
        for s in range(2):
            load_b(t, s, s).start()
        lam = lam_l[t, 0:1, 0:1]

        def piece(p, _):
            cols = rows_of(p, CH)
            s = lax.rem(p, 2)
            gt[...] = contract(left[...], right[:, cols], 0, 0)
            load_b(t, p, s).wait()

            def inner(i, _):
                rr = rows_of(i, STEP_D)
                w, b = ws[t][rr, cols].astype(F32), cin[s, rr].astype(F32)
                g = gt[rr] * (1.0 / TOK)
                new_b = 0.9 * b + 0.1 * g
                new_w = w - 0.5 * (0.3 * g + 0.7 * new_b)
                ws[t][rr, cols] = jnp.where(lam > 0.5, new_w, new_b).astype(BF16)
                return 0

            def part(h, _):
                lax.fori_loop(h * (PART // STEP_D), (h + 1) * (PART // STEP_D), inner, 0)
                p_copy(t, p, h).start()
                return 0

            lax.fori_loop(0, PARTS, part, 0)

            @pl.when(p + 2 < NP)
            def _():
                load_b(t, p + 2, s).start()

            return 0

        lax.fori_loop(0, NP, piece, 0)

    ag_wait(0)
    step_matrix(0, hid, gs)

    for d in (1, 2, 3):
        rs_copy(2, stg.at[0, d - 1], d).wait()

    def make_grads(i, _):
        rr = rows_of(i, STEP)
        back = ((own_b[rr] + rcv[2, 0, rr]) + rcv[2, 1, rr]) + rcv[2, 2, rr]
        gate, up = stg[0, 3, rr], stg[1, 3, rr]
        sig = jax.nn.sigmoid(gate)
        wr = pl.ds(pl.multiple_of(x * CH + i * STEP, STEP), STEP)
        dgt[wr] = (back * up * sig * (1.0 + gate * (1.0 - sig))).astype(BF16)
        dup[wr] = (back * (gate * sig)).astype(BF16)
        return 0

    lax.fori_loop(0, CH // STEP, make_grads, 0)
    for t in (1, 2):
        for d in (1, 2, 3):
            ag_copy(t, d).start()

    def token_part(grads, w_ref, first):
        def step(j, _):
            part = jnp.dot(grads[rows_of(j, CH)], w_ref[...], preferred_element_type=F32)
            part = part.reshape(2, 2, BLK, D)
            two = rows_of(j, 2)
            if first:
                tp[two] = part
            else:
                tp[two] = tp[two] + part
            return 0

        lax.fori_loop(0, 4, step, 0)

    ag_wait(1)
    token_part(dgt, wg, True)
    step_matrix(1, dgt, xs)
    ag_wait(2)
    token_part(dup, wu, False)
    tc_copy = remote(tp.at[:, 1 - k], tc, tc_s.at[0], tc_s.at[1], sib)
    tc_copy.start()
    step_matrix(2, dup, xs)

    lam_copy.wait()

    def means(t, q_a, p_a, q_b, p_b):
        la = rebuild(lam_l[t, 0:1, 0:1])
        lb = rebuild(lam_r[t, 0:1, 0:1])
        q_a, p_a, q_b, p_b = (v.astype(F32) for v in (q_a, p_a, q_b, p_b))
        w = (la[0] * q_a + la[1] * p_a) + (lb[0] * q_b + lb[1] * p_b)
        b = (la[2] * q_a + la[3] * p_a) + (lb[2] * q_b + lb[3] * p_b)
        return (0.5 * w).astype(BF16), (0.5 * b).astype(BF16)

    def load_q(t, p, s):
        return pltpu.make_async_copy(qr.at[t * NP + p], cin.at[s], cin_s.at[s])

    def combine(t):
        for s in range(2):
            q_copy(t, s).wait()
            load_q(t, s, s).start()

        def piece(p, _):
            s = lax.rem(p, 2)
            i = t * NP + p
            cols = rows_of(p, CH)
            load_q(t, p, s).wait()

            def inner(n, _):
                rr = rows_of(n, STEP_D)
                w, b = means(t, qs[t][rr, cols], ws[t][rr, cols], cin[s, rr], pr[i, rr])
                ws[t][rr, cols] = w
                qs[t][rr, cols] = b
                return 0

            def part(h, _):
                p_copy(t, p, h).wait()
                return lax.fori_loop(h * (PART // STEP_D), (h + 1) * (PART // STEP_D), inner, 0)

            lax.fori_loop(0, PARTS, part, 0)

            @pl.when(p + 2 < NP)
            def _():
                q_copy(t, p + 2).wait()
                load_q(t, p + 2, s).start()

            return 0

        lax.fori_loop(0, NP, piece, 0)

    tc_copy.wait()

    def add_core(i, _):
        tc[i] = tc[i] + tp[i, k]
        return 0

    lax.fori_loop(0, 8, add_core, 0)

    def ty_copy(d, half):
        to = half * 4 + lax.rem(y + d, 4)
        return remote(tc.at[to], ty.at[d - 1, half], ty_s.at[d - 1, half], ty_r.at[d - 1, half], ydev[d])

    for d in (1, 2, 3):
        for half in range(2):
            ty_copy(d, half).start()

    combine(0)

    for d in (1, 2, 3):
        for half in range(2):
            ty_copy(d, half).wait()

    def along_y(half):
        return ((tc[half * 4 + y] + ty[0, half]) + ty[1, half]) + ty[2, half]

    tzs[...] = along_y(1 - zl).astype(BF16)
    tz_copy = remote(tzs, tz, tz_s.at[0], tz_s.at[1], zn)
    tz_copy.start()

    combine(1)
    combine(2)

    tz_copy.wait()
    tgo[...] = (along_y(zl) + tz[...].astype(F32)).astype(BF16)

    for m in range(2):
        for owner, n, dev in sends[m]:
            tok(m, owner, n, dev).wait_send()
    for t in range(3):
        for d in (1, 2, 3):
            ag_copy(t, d).wait_send()


def flush_kernel(*refs):
    n = len(refs) // 2
    copies = [pltpu.make_async_copy(refs[i], refs[n + i], refs[-1].at[i]) for i in range(n)]
    for cp in copies:
        cp.start()
    for cp in copies:
        cp.wait()


def flush(arrays):
    return pl.pallas_call(
        flush_kernel,
        out_shape=[jax.ShapeDtypeStruct(a.shape, a.dtype) for a in arrays],
        in_specs=[pl.BlockSpec(memory_space=pltpu.VMEM)] * len(arrays),
        out_specs=[pl.BlockSpec(memory_space=pl.ANY)] * len(arrays),
        scratch_shapes=[pltpu.SemaphoreType.DMA((len(arrays),))],
        compiler_params=pltpu.CompilerParams(vmem_limit_bytes=2**20),
    )(*[pltpu.with_memory_space_constraint(a, pltpu.VMEM) for a in arrays])


def body(tokens, grad_out, wg, wu, wd, bg, bu, bd):
    dma = pltpu.SemaphoreType.DMA
    whole = [(BLK, D)] + [(F, D)] * 6
    scratch = [
        pltpu.VMEM((TOK, D), BF16),
        pltpu.VMEM((TOK, D), BF16),
        pltpu.VMEM((3 * NP, F, CH), BF16),
        pltpu.VMEM((2, 4, CH, F), F32),
        pltpu.VMEM((CH, F), F32),
        pltpu.VMEM((3, 3, CH, F), F32),
        pltpu.VMEM((TOK, F), BF16),
        pltpu.VMEM((TOK, F), BF16),
        pltpu.VMEM((TOK, F), BF16),
        pltpu.VMEM((8, 2, BLK, D), F32),
        pltpu.VMEM((8, BLK, D), F32),
        pltpu.VMEM((3, 2, BLK, D), F32),
        pltpu.VMEM((BLK, D), BF16),
        pltpu.VMEM((BLK, D), BF16),
        pltpu.VMEM((F, CH), F32),
        pltpu.VMEM((2, F, CH), BF16),
        pltpu.VMEM((3, 8, 128), F32),
        pltpu.VMEM((3, 8, 128), F32),
        dma((5,)),
        dma((2,)),
        dma((2, 15)),
        dma((2, 16)),
        dma((3 * NP,)),
        dma((3 * NP,)),
        dma((3 * NP, PARTS)),
        dma((3 * NP, PARTS)),
        dma((2,)),
        dma((3, 3)),
        dma((3, 3)),
        dma((3, 3)),
        dma((3, 3)),
        dma((2,)),
        dma((3, 2)),
        dma((3, 2)),
        dma((2,)),
        dma((2,)),
    ]
    res = pl.pallas_call(
        kernel,
        out_shape=[pltpu.VMEM(s, BF16) for s in whole] + [jax.ShapeDtypeStruct((3 * NP, F, CH), BF16)],
        in_specs=[pl.BlockSpec(memory_space=pl.ANY)] * 8,
        out_specs=[pl.BlockSpec(memory_space=pltpu.VMEM)] * 7 + [pl.BlockSpec(memory_space=pl.ANY)],
        scratch_shapes=scratch,
        compiler_params=pltpu.CompilerParams(
            collective_id=0, has_side_effects=True, vmem_limit_bytes=48 * 2**20
        ),
        cost_estimate=pl.CostEstimate(
            flops=16 * TOK * D * F, bytes_accessed=40 * D * F, transcendentals=2 * CH * F
        ),
    )(tokens, grad_out, wg[0].T, wu[0].T, wd[0], bg[0].T, bu[0].T, bd[0])
    tg, gw, uw, dw, gb, ub, db = flush(res[:7])
    return tg, gw.T, uw.T, dw, gb.T, ub.T, db


def solution(mesh):
    weights = (P("rep", "row", "col"), P("rep", "row", "col"), P("rep", "col", "row"))
    means = (P("row", "col"), P("row", "col"), P("col", "row"))
    return jax.shard_map(
        body,
        mesh=mesh,
        in_specs=(P(("rep", "col"), "row"),) * 2 + weights * 2,
        out_specs=(P(("rep", "col"), "row"),) + means * 2,
        check_vma=False,
    )
```

```python
import functools

import jax
import jax.numpy as jnp
from jax import lax
from jax.experimental import pallas as pl
from jax.experimental.pallas import tpu as pltpu
from jax.sharding import PartitionSpec as P

MESH = pl.DeviceIdType.MESH
F32, BF16 = jnp.float32, jnp.bfloat16

TOK = 1024
D = 1280
F = 864
BLK = 64
CH = 256
NP = D // CH
PARTS = 3
PART = F // PARTS
STEP = 16
STEP_D = 48
MIX = 1.85
LEAD = 1.35


def rows_of(i, n):
    return pl.ds(pl.multiple_of(i * n, n), n)


def contract(a, b, dim_a, dim_b):
    return lax.dot_general(
        a, b, (((dim_a,), (dim_b,)), ((), ())), preferred_element_type=F32
    )


def rebuild(lam):
    keep = 1.0 - lam
    return keep, lam - MIX * keep, lam / MIX, keep - lam / MIX


def kernel(
    x_in, g_in, wg_in, wu_in, wd_in, bg_in, bu_in, bd_in,
    tgo, wg, wu, wd, qg, qu, qd, qr,
    xs, gs, pr, stg, own_b, rcv, hid, dgt, dup,
    tp, tc, ty, tzs, tz, gt, cin, lam_l, lam_r,
    ld_s, b_s, tok_s, tok_r, q_s, q_r, p_s, p_r, lam_s, rs_s, rs_r, ag_s, ag_r,
    tc_s, ty_s, ty_r, tz_s, cin_s,
):
    r, x, c = lax.axis_index("rep"), lax.axis_index("row"), lax.axis_index("col")
    k = lax.rem(c, 2)
    y = lax.rem(c // 2, 4)
    zl = c // 8

    ws, qs = (wd, wg, wu), (qd, qg, qu)

    def col_of(zl_, y_, k_):
        return zl_ * 8 + y_ * 2 + k_

    peer = (1 - r, x, c)
    sib = (r, x, col_of(zl, y, 1 - k))
    zn = (r, x, col_of(1 - zl, y, k))
    ydev = {d: (r, x, col_of(zl, lax.rem(y + d, 4), k)) for d in (1, 2, 3)}

    def xdev(d):
        return (r, lax.rem(x + d, 4), c)

    bar = pltpu.get_barrier_semaphore()
    partners = [peer, sib, zn] + [ydev[d] for d in (1, 2, 3)] + [xdev(d) for d in (1, 2, 3)]
    for dev in partners:
        pl.semaphore_signal(bar, 1, device_id=dev, device_id_type=MESH)

    def load(src, dst, i):
        return pltpu.make_async_copy(src, dst, ld_s.at[i])

    own_rows = rows_of(c, BLK)
    loads = [
        load(x_in, xs.at[own_rows], 0),
        load(g_in, gs.at[own_rows], 1),
        load(wd_in, wd, 2),
        load(wg_in, wg, 3),
        load(wu_in, wu, 4),
    ]
    for cp in loads:
        cp.start()

    bs = (bd_in, bg_in, bu_in)

    def load_b(t, p, s):
        return pltpu.make_async_copy(bs[t].at[:, rows_of(p, CH)], cin.at[s], b_s.at[s])

    for s in range(2):
        load_b(0, s, s).start()

    def remote(src, dst, ss, rs, dev):
        return pltpu.make_async_remote_copy(
            src_ref=src, dst_ref=dst, send_sem=ss, recv_sem=rs, device_id=dev, device_id_type=MESH
        )

    mats = (xs, gs)

    def tok(m, owner, n, dev):
        blk = mats[m].at[rows_of(owner, BLK)]
        return remote(blk, blk, tok_s.at[m, n], tok_r.at[m, owner], dev)

    zn_owner = col_of(1 - zl, y, k)
    y_owner = {d: col_of(zl, lax.rem(y + 4 - d, 4), k) for d in (1, 2, 3)}
    zy_owner = {d: col_of(1 - zl, lax.rem(y + 4 - d, 4), k) for d in (1, 2, 3)}

    def tok_list(m):
        return (
            [(c, 1, zn), (c, 0, sib)]
            + [(c, 1 + d, ydev[d]) for d in (1, 2, 3)]
            + [(zn_owner, 5 + d, ydev[d]) for d in (1, 2, 3)]
            + [(zn_owner, 5, sib)]
            + [(y_owner[d], 8 + d, sib) for d in (1, 2, 3)]
            + [(zy_owner[d], 11 + d, sib) for d in (1, 2, 3)]
        )

    sends = [tok_list(0), tok_list(1)]

    def tok_start(m, lo, hi):
        for owner, n, dev in sends[m][lo:hi]:
            tok(m, owner, n, dev).start()

    def tok_wait(m, owner):
        tok(m, owner, 0, sib).wait_recv()

    def squares(w, b):
        u = w - 0.315 * b
        v = (0.9 * MIX) * b
        return u * u, v * v

    def fold(v):
        return jnp.sum(v.reshape(STEP_D // 8, 8, CH), axis=0)

    def q_copy(t, p):
        i = t * NP + p
        return remote(qs[t].at[:, rows_of(p, CH)], qr.at[i], q_s.at[i], q_r.at[i], peer)

    def q_piece(t, p, carry):
        s = lax.rem(p, 2)
        cols = rows_of(p, CH)
        load_b(t, p, s).wait()

        def inner(i, acc):
            rr = rows_of(i, STEP_D)
            w = ws[t][rr, cols].astype(F32)
            b = cin[s, rr].astype(F32)
            qs[t][rr, cols] = (w + LEAD * b).astype(BF16)
            uu, vv = squares(w, b)
            return acc[0] + fold(uu), acc[1] + fold(vv)

        return lax.fori_loop(0, F // STEP_D, inner, carry)

    def q_next(t, p):
        q_copy(t, p).start()

        @pl.when(p + 2 < NP)
        def _():
            load_b(t, p + 2, lax.rem(p, 2)).start()

    def choose(t, su, sv):
        lam = (jnp.sum(sv, keepdims=True) > jnp.sum(su, keepdims=True)).astype(F32)
        lam_l[t] = jnp.broadcast_to(lam, (8, 128))

    def q_rest(t, p, carry):
        carry = q_piece(t, p, carry)
        q_next(t, p)
        return carry

    zero = jnp.zeros((8, CH), F32)
    loads[2].wait()
    carry = q_piece(0, jnp.int32(0), (zero, zero))
    pl.semaphore_wait(bar, len(partners))
    loads[0].wait()
    tok_start(0, 0, 5)
    loads[1].wait()
    tok_start(1, 0, 1)
    q_next(0, jnp.int32(0))
    choose(0, *lax.fori_loop(1, NP, functools.partial(q_rest, 0), carry))
    for t in (1, 2):
        for s in range(2):
            load_b(t, s, s).start()
        loads[2 + t].wait()
        choose(t, *lax.fori_loop(0, NP, functools.partial(q_rest, t), (zero, zero)))
    lam_copy = remote(lam_l, lam_r, lam_s.at[0], lam_s.at[1], peer)
    lam_copy.start()

    def forward_near(m):
        tok_wait(m, zn_owner)
        tok_start(m, 5, 9)
        for i, d in enumerate((1, 2, 3)):
            tok_wait(m, y_owner[d])
            tok_start(m, 9 + i, 10 + i)

    def forward_far(m):
        for i, d in enumerate((1, 2, 3)):
            tok_wait(m, zy_owner[d])
            tok_start(m, 12 + i, 13 + i)

    def from_sibling(m):
        for i in range(8):
            tok_wait(m, 2 * i + 1 - k)

    forward_near(0)
    tok_start(1, 1, 5)
    forward_far(0)
    from_sibling(0)

    def rs_copy(t, src, d):
        return remote(src, rcv.at[t, d - 1], rs_s.at[t, d - 1], rs_r.at[t, d - 1], xdev(d))

    def partial_in(t, w_ref):
        def step(i, _):
            j = lax.rem(x + i + 1, 4)
            stg[t, i] = contract(xs[rows_of(j, CH)], w_ref[...], 1, 1)

            @pl.when(i < 3)
            def _():
                rs_copy(t, stg.at[t, i], i + 1).start()

            return 0

        lax.fori_loop(0, 4, step, 0)

    partial_in(0, wg)
    forward_near(1)
    partial_in(1, wu)
    forward_far(1)
    from_sibling(1)

    for t in range(2):
        for d in (1, 2, 3):
            rs_copy(t, stg.at[t, d - 1], d).wait()

    def ag_copy(t, d, start=True):
        ref = (hid, dgt, dup)[t]
        rr = rows_of(x, CH)
        return remote(ref.at[rr], ref.at[rr], ag_s.at[t, d - 1], ag_r.at[t, d - 1], xdev(d))

    def ag_wait(t):
        ref = (hid, dgt, dup)[t]
        for d in (1, 2, 3):
            rr = rows_of(lax.rem(x + 4 - d, 4), CH)
            remote(ref.at[rr], ref.at[rr], ag_s.at[t, d - 1], ag_r.at[t, d - 1], xdev(d)).wait_recv()

    def make_hidden(i, _):
        rr = rows_of(i, STEP)
        gate = ((stg[0, 3, rr] + rcv[0, 0, rr]) + rcv[0, 1, rr]) + rcv[0, 2, rr]
        up = ((stg[1, 3, rr] + rcv[1, 0, rr]) + rcv[1, 1, rr]) + rcv[1, 2, rr]
        sig = jax.nn.sigmoid(gate)
        stg[0, 3, rr] = gate
        stg[1, 3, rr] = up
        hid[pl.ds(pl.multiple_of(x * CH + i * STEP, STEP), STEP)] = (gate * sig * up).astype(BF16)
        return 0

    lax.fori_loop(0, CH // STEP, make_hidden, 0)
    for d in (1, 2, 3):
        ag_copy(0, d).start()

    def partial_back(i, _):
        j = lax.rem(x + i + 1, 4)
        stg[0, i] = contract(gs[rows_of(j, CH)], wd[...], 1, 1)
        rs_copy(2, stg.at[0, i], i + 1).start()
        return 0

    lax.fori_loop(0, 3, partial_back, 0)
    own_b[...] = contract(gs[rows_of(x, CH)], wd[...], 1, 1)

    def p_copy(t, p, h):
        i = t * NP + p
        rr = rows_of(h, PART)
        return remote(ws[t].at[rr, rows_of(p, CH)], pr.at[i, rr], p_s.at[i, h], p_r.at[i, h], peer)

    def step_matrix(t, left, right):
        for s in range(2):
            load_b(t, s, s).start()
        lam = lam_l[t, 0:1, 0:1]

        def piece(p, _):
            cols = rows_of(p, CH)
            s = lax.rem(p, 2)
            gt[...] = contract(left[...], right[:, cols], 0, 0)
            load_b(t, p, s).wait()

            def inner(i, _):
                rr = rows_of(i, STEP_D)
                w, b = ws[t][rr, cols].astype(F32), cin[s, rr].astype(F32)
                g = gt[rr] * (1.0 / TOK)
                new_b = 0.9 * b + 0.1 * g
                new_w = w - 0.5 * (0.3 * g + 0.7 * new_b)
                ws[t][rr, cols] = jnp.where(lam > 0.5, new_w, new_b).astype(BF16)
                return 0

            def part(h, _):
                lax.fori_loop(h * (PART // STEP_D), (h + 1) * (PART // STEP_D), inner, 0)
                p_copy(t, p, h).start()
                return 0

            lax.fori_loop(0, PARTS, part, 0)

            @pl.when(p + 2 < NP)
            def _():
                load_b(t, p + 2, s).start()

            return 0

        lax.fori_loop(0, NP, piece, 0)

    ag_wait(0)
    step_matrix(0, hid, gs)

    for d in (1, 2, 3):
        rs_copy(2, stg.at[0, d - 1], d).wait()

    def make_grads(i, _):
        rr = rows_of(i, STEP)
        back = ((own_b[rr] + rcv[2, 0, rr]) + rcv[2, 1, rr]) + rcv[2, 2, rr]
        gate, up = stg[0, 3, rr], stg[1, 3, rr]
        sig = jax.nn.sigmoid(gate)
        wr = pl.ds(pl.multiple_of(x * CH + i * STEP, STEP), STEP)
        dgt[wr] = (back * up * sig * (1.0 + gate * (1.0 - sig))).astype(BF16)
        dup[wr] = (back * (gate * sig)).astype(BF16)
        return 0

    lax.fori_loop(0, CH // STEP, make_grads, 0)
    for t in (1, 2):
        for d in (1, 2, 3):
            ag_copy(t, d).start()

    def token_part(grads, w_ref, first):
        def step(j, _):
            part = jnp.dot(grads[rows_of(j, CH)], w_ref[...], preferred_element_type=F32)
            part = part.reshape(2, 2, BLK, D)
            two = rows_of(j, 2)
            if first:
                tp[two] = part
            else:
                tp[two] = tp[two] + part
            return 0

        lax.fori_loop(0, 4, step, 0)

    ag_wait(1)
    token_part(dgt, wg, True)
    step_matrix(1, dgt, xs)
    ag_wait(2)
    token_part(dup, wu, False)
    tc_copy = remote(tp.at[:, 1 - k], tc, tc_s.at[0], tc_s.at[1], sib)
    tc_copy.start()
    step_matrix(2, dup, xs)

    lam_copy.wait()

    def means(t, q_a, p_a, q_b, p_b):
        la = rebuild(lam_l[t, 0:1, 0:1])
        lb = rebuild(lam_r[t, 0:1, 0:1])
        q_a, p_a, q_b, p_b = (v.astype(F32) for v in (q_a, p_a, q_b, p_b))
        w = (la[0] * q_a + la[1] * p_a) + (lb[0] * q_b + lb[1] * p_b)
        b = (la[2] * q_a + la[3] * p_a) + (lb[2] * q_b + lb[3] * p_b)
        return (0.5 * w).astype(BF16), (0.5 * b).astype(BF16)

    def load_q(t, p, s):
        return pltpu.make_async_copy(qr.at[t * NP + p], cin.at[s], cin_s.at[s])

    def combine(t):
        for s in range(2):
            q_copy(t, s).wait()
            load_q(t, s, s).start()

        def piece(p, _):
            s = lax.rem(p, 2)
            i = t * NP + p
            cols = rows_of(p, CH)
            load_q(t, p, s).wait()

            def inner(n, _):
                rr = rows_of(n, STEP_D)
                w, b = means(t, qs[t][rr, cols], ws[t][rr, cols], cin[s, rr], pr[i, rr])
                ws[t][rr, cols] = w
                qs[t][rr, cols] = b
                return 0

            def part(h, _):
                p_copy(t, p, h).wait()
                return lax.fori_loop(h * (PART // STEP_D), (h + 1) * (PART // STEP_D), inner, 0)

            lax.fori_loop(0, PARTS, part, 0)

            @pl.when(p + 2 < NP)
            def _():
                q_copy(t, p + 2).wait()
                load_q(t, p + 2, s).start()

            return 0

        lax.fori_loop(0, NP, piece, 0)

    tc_copy.wait()

    def add_core(i, _):
        tc[i] = tc[i] + tp[i, k]
        return 0

    lax.fori_loop(0, 8, add_core, 0)

    def ty_copy(d, half):
        to = half * 4 + lax.rem(y + d, 4)
        return remote(tc.at[to], ty.at[d - 1, half], ty_s.at[d - 1, half], ty_r.at[d - 1, half], ydev[d])

    for d in (1, 2, 3):
        for half in range(2):
            ty_copy(d, half).start()

    combine(0)

    for d in (1, 2, 3):
        for half in range(2):
            ty_copy(d, half).wait()

    def along_y(half):
        return ((tc[half * 4 + y] + ty[0, half]) + ty[1, half]) + ty[2, half]

    tzs[...] = along_y(1 - zl).astype(BF16)
    tz_copy = remote(tzs, tz, tz_s.at[0], tz_s.at[1], zn)
    tz_copy.start()

    combine(1)

    mine = zl * 4 + y
    tc[mine] = along_y(zl)
    for m in range(2):
        for owner, n, dev in sends[m]:
            tok(m, owner, n, dev).wait_send()
    for t in range(3):
        for d in (1, 2, 3):
            ag_copy(t, d).wait_send()

    combine(2)

    tz_copy.wait()
    tgo[...] = (tc[mine] + tz[...].astype(F32)).astype(BF16)


def flush_kernel(*refs):
    n = len(refs) // 2
    copies = [pltpu.make_async_copy(refs[i], refs[n + i], refs[-1].at[i]) for i in range(n)]
    for cp in copies:
        cp.start()
    for cp in copies:
        cp.wait()


def flush(arrays):
    return pl.pallas_call(
        flush_kernel,
        out_shape=[jax.ShapeDtypeStruct(a.shape, a.dtype) for a in arrays],
        in_specs=[pl.BlockSpec(memory_space=pltpu.VMEM)] * len(arrays),
        out_specs=[pl.BlockSpec(memory_space=pl.ANY)] * len(arrays),
        scratch_shapes=[pltpu.SemaphoreType.DMA((len(arrays),))],
        compiler_params=pltpu.CompilerParams(vmem_limit_bytes=2**20),
    )(*[pltpu.with_memory_space_constraint(a, pltpu.VMEM) for a in arrays])


def body(tokens, grad_out, wg, wu, wd, bg, bu, bd):
    dma = pltpu.SemaphoreType.DMA
    whole = [(BLK, D)] + [(F, D)] * 6
    scratch = [
        pltpu.VMEM((TOK, D), BF16),
        pltpu.VMEM((TOK, D), BF16),
        pltpu.VMEM((3 * NP, F, CH), BF16),
        pltpu.VMEM((2, 4, CH, F), F32),
        pltpu.VMEM((CH, F), F32),
        pltpu.VMEM((3, 3, CH, F), F32),
        pltpu.VMEM((TOK, F), BF16),
        pltpu.VMEM((TOK, F), BF16),
        pltpu.VMEM((TOK, F), BF16),
        pltpu.VMEM((8, 2, BLK, D), F32),
        pltpu.VMEM((8, BLK, D), F32),
        pltpu.VMEM((3, 2, BLK, D), F32),
        pltpu.VMEM((BLK, D), BF16),
        pltpu.VMEM((BLK, D), BF16),
        pltpu.VMEM((F, CH), F32),
        pltpu.VMEM((2, F, CH), BF16),
        pltpu.VMEM((3, 8, 128), F32),
        pltpu.VMEM((3, 8, 128), F32),
        dma((5,)),
        dma((2,)),
        dma((2, 15)),
        dma((2, 16)),
        dma((3 * NP,)),
        dma((3 * NP,)),
        dma((3 * NP, PARTS)),
        dma((3 * NP, PARTS)),
        dma((2,)),
        dma((3, 3)),
        dma((3, 3)),
        dma((3, 3)),
        dma((3, 3)),
        dma((2,)),
        dma((3, 2)),
        dma((3, 2)),
        dma((2,)),
        dma((2,)),
    ]
    res = pl.pallas_call(
        kernel,
        out_shape=[pltpu.VMEM(s, BF16) for s in whole] + [jax.ShapeDtypeStruct((3 * NP, F, CH), BF16)],
        in_specs=[pl.BlockSpec(memory_space=pl.ANY)] * 8,
        out_specs=[pl.BlockSpec(memory_space=pltpu.VMEM)] * 7 + [pl.BlockSpec(memory_space=pl.ANY)],
        scratch_shapes=scratch,
        compiler_params=pltpu.CompilerParams(
            collective_id=0, has_side_effects=True, vmem_limit_bytes=48 * 2**20
        ),
        cost_estimate=pl.CostEstimate(
            flops=16 * TOK * D * F, bytes_accessed=40 * D * F, transcendentals=2 * CH * F
        ),
    )(tokens, grad_out, wg[0].T, wu[0].T, wd[0], bg[0].T, bu[0].T, bd[0])
    tg, gw, uw, dw, gb, ub, db = flush(res[:7])
    return tg, gw.T, uw.T, dw, gb.T, ub.T, db


def solution(mesh):
    weights = (P("rep", "row", "col"), P("rep", "row", "col"), P("rep", "col", "row"))
    means = (P("row", "col"), P("row", "col"), P("col", "row"))
    return jax.shard_map(
        body,
        mesh=mesh,
        in_specs=(P(("rep", "col"), "row"),) * 2 + weights * 2,
        out_specs=(P(("rep", "col"), "row"),) + means * 2,
        check_vma=False,
    )
```

```python
import functools

import jax
import jax.numpy as jnp
from jax import lax
from jax.experimental import pallas as pl
from jax.experimental.pallas import tpu as pltpu
from jax.sharding import PartitionSpec as P

MESH = pl.DeviceIdType.MESH
F32, BF16 = jnp.float32, jnp.bfloat16

TOK = 1024
D = 1280
F = 864
BLK = 64
CH = 256
NP = D // CH
PARTS = 3
PART = F // PARTS
STEP = 16
STEP_D = 48
MIX = 1.85
LEAD = 1.35


def rows_of(i, n):
    return pl.ds(pl.multiple_of(i * n, n), n)


def contract(a, b, dim_a, dim_b):
    return lax.dot_general(
        a, b, (((dim_a,), (dim_b,)), ((), ())), preferred_element_type=F32
    )


def rebuild(lam):
    keep = 1.0 - lam
    return keep, lam - MIX * keep, lam / MIX, keep - lam / MIX


def kernel(
    x_in, g_in, wg_in, wu_in, wd_in, bg_in, bu_in, bd_in,
    tgo, wg, wu, wd, qg, qu, qd, qr,
    xs, gs, pr, stg, own_b, rcv, hid, dgt, dup,
    tp, tc, ty, tzs, tz, gt, cin, lam_l, lam_r,
    ld_s, b_s, tok_s, tok_r, q_s, q_r, p_s, p_r, lam_s, rs_s, rs_r, ag_s, ag_r,
    tc_s, ty_s, ty_r, tz_s, cin_s,
):
    r, x, c = lax.axis_index("rep"), lax.axis_index("row"), lax.axis_index("col")
    k = lax.rem(c, 2)
    y = lax.rem(c // 2, 4)
    zl = c // 8

    ws, qs = (wd, wg, wu), (qd, qg, qu)

    def col_of(zl_, y_, k_):
        return zl_ * 8 + y_ * 2 + k_

    peer = (1 - r, x, c)
    sib = (r, x, col_of(zl, y, 1 - k))
    zn = (r, x, col_of(1 - zl, y, k))
    ydev = {d: (r, x, col_of(zl, lax.rem(y + d, 4), k)) for d in (1, 2, 3)}

    def xdev(d):
        return (r, lax.rem(x + d, 4), c)

    bar = pltpu.get_barrier_semaphore()
    partners = [peer, sib, zn] + [ydev[d] for d in (1, 2, 3)] + [xdev(d) for d in (1, 2, 3)]
    for dev in partners:
        pl.semaphore_signal(bar, 1, device_id=dev, device_id_type=MESH)

    def load(src, dst, i):
        return pltpu.make_async_copy(src, dst, ld_s.at[i])

    own_rows = rows_of(c, BLK)
    loads = [
        load(x_in, xs.at[own_rows], 0),
        load(g_in, gs.at[own_rows], 1),
        load(wd_in, wd, 2),
        load(wg_in, wg, 3),
        load(wu_in, wu, 4),
    ]
    loads[2].start()

    bs = (bd_in, bg_in, bu_in)

    def load_b(t, p, s):
        return pltpu.make_async_copy(bs[t].at[:, rows_of(p, CH)], cin.at[s], b_s.at[s])

    for s in range(2):
        load_b(0, s, s).start()
    for i in (0, 1, 3, 4):
        loads[i].start()

    def remote(src, dst, ss, rs, dev):
        return pltpu.make_async_remote_copy(
            src_ref=src, dst_ref=dst, send_sem=ss, recv_sem=rs, device_id=dev, device_id_type=MESH
        )

    mats = (xs, gs)

    def tok(m, owner, n, dev):
        blk = mats[m].at[rows_of(owner, BLK)]
        src = (x_in, g_in)[m] if n < 5 else blk
        return remote(src, blk, tok_s.at[m, n], tok_r.at[m, owner], dev)

    zn_owner = col_of(1 - zl, y, k)
    y_owner = {d: col_of(zl, lax.rem(y + 4 - d, 4), k) for d in (1, 2, 3)}
    zy_owner = {d: col_of(1 - zl, lax.rem(y + 4 - d, 4), k) for d in (1, 2, 3)}

    def tok_list(m):
        return (
            [(c, 1, zn), (c, 0, sib)]
            + [(c, 1 + d, ydev[d]) for d in (1, 2, 3)]
            + [(zn_owner, 5 + d, ydev[d]) for d in (1, 2, 3)]
            + [(zn_owner, 5, sib)]
            + [(y_owner[d], 8 + d, sib) for d in (1, 2, 3)]
            + [(zy_owner[d], 11 + d, sib) for d in (1, 2, 3)]
        )

    sends = [tok_list(0), tok_list(1)]

    def tok_start(m, lo, hi):
        for owner, n, dev in sends[m][lo:hi]:
            tok(m, owner, n, dev).start()

    def tok_wait(m, owner):
        tok(m, owner, 0, sib).wait_recv()

    def squares(w, b):
        u = w - 0.315 * b
        v = (0.9 * MIX) * b
        return u * u, v * v

    def fold(v):
        return jnp.sum(v.reshape(STEP_D // 8, 8, CH), axis=0)

    def q_copy(t, p):
        i = t * NP + p
        return remote(qs[t].at[:, rows_of(p, CH)], qr.at[i], q_s.at[i], q_r.at[i], peer)

    def q_piece(t, p, carry):
        s = lax.rem(p, 2)
        cols = rows_of(p, CH)
        load_b(t, p, s).wait()

        def inner(i, acc):
            rr = rows_of(i, STEP_D)
            w = ws[t][rr, cols].astype(F32)
            b = cin[s, rr].astype(F32)
            qs[t][rr, cols] = (w + LEAD * b).astype(BF16)
            uu, vv = squares(w, b)
            return acc[0] + fold(uu), acc[1] + fold(vv)

        return lax.fori_loop(0, F // STEP_D, inner, carry)

    def q_next(t, p):
        q_copy(t, p).start()

        @pl.when(p + 2 < NP)
        def _():
            load_b(t, p + 2, lax.rem(p, 2)).start()

    def choose(t, su, sv):
        lam = (jnp.sum(sv, keepdims=True) > jnp.sum(su, keepdims=True)).astype(F32)
        lam_l[t] = jnp.broadcast_to(lam, (8, 128))

    def q_rest(t, p, carry):
        carry = q_piece(t, p, carry)
        q_next(t, p)
        return carry

    zero = jnp.zeros((8, CH), F32)
    pl.semaphore_wait(bar, len(partners))
    for m in range(2):
        tok_start(m, 0, 1)
    tok_start(0, 1, 5)
    for t in range(3):
        if t:
            for s in range(2):
                load_b(t, s, s).start()
        loads[2 + t].wait()
        choose(t, *lax.fori_loop(0, NP, functools.partial(q_rest, t), (zero, zero)))
    lam_copy = remote(lam_l, lam_r, lam_s.at[0], lam_s.at[1], peer)
    lam_copy.start()

    def forward_near(m):
        tok_wait(m, zn_owner)
        tok_start(m, 5, 9)
        for i, d in enumerate((1, 2, 3)):
            tok_wait(m, y_owner[d])
            tok_start(m, 9 + i, 10 + i)

    def forward_far(m):
        for i, d in enumerate((1, 2, 3)):
            tok_wait(m, zy_owner[d])
            tok_start(m, 12 + i, 13 + i)

    def from_sibling(m):
        for i in range(8):
            tok_wait(m, 2 * i + 1 - k)

    forward_near(0)
    tok_start(1, 1, 5)
    forward_far(0)
    from_sibling(0)
    loads[0].wait()

    def rs_copy(t, src, d):
        return remote(src, rcv.at[t, d - 1], rs_s.at[t, d - 1], rs_r.at[t, d - 1], xdev(d))

    def partial_in(t, w_ref):
        def step(i, _):
            j = lax.rem(x + i + 1, 4)
            stg[t, i] = contract(xs[rows_of(j, CH)], w_ref[...], 1, 1)

            @pl.when(i < 3)
            def _():
                rs_copy(t, stg.at[t, i], i + 1).start()

            return 0

        lax.fori_loop(0, 4, step, 0)

    partial_in(0, wg)
    forward_near(1)
    partial_in(1, wu)
    forward_far(1)
    from_sibling(1)
    loads[1].wait()

    for t in range(2):
        for d in (1, 2, 3):
            rs_copy(t, stg.at[t, d - 1], d).wait()

    def ag_copy(t, d, start=True):
        ref = (hid, dgt, dup)[t]
        rr = rows_of(x, CH)
        return remote(ref.at[rr], ref.at[rr], ag_s.at[t, d - 1], ag_r.at[t, d - 1], xdev(d))

    def ag_wait(t):
        ref = (hid, dgt, dup)[t]
        for d in (1, 2, 3):
            rr = rows_of(lax.rem(x + 4 - d, 4), CH)
            remote(ref.at[rr], ref.at[rr], ag_s.at[t, d - 1], ag_r.at[t, d - 1], xdev(d)).wait_recv()

    def make_hidden(i, _):
        rr = rows_of(i, STEP)
        gate = ((stg[0, 3, rr] + rcv[0, 0, rr]) + rcv[0, 1, rr]) + rcv[0, 2, rr]
        up = ((stg[1, 3, rr] + rcv[1, 0, rr]) + rcv[1, 1, rr]) + rcv[1, 2, rr]
        sig = jax.nn.sigmoid(gate)
        stg[0, 3, rr] = gate
        stg[1, 3, rr] = up
        hid[pl.ds(pl.multiple_of(x * CH + i * STEP, STEP), STEP)] = (gate * sig * up).astype(BF16)
        return 0

    lax.fori_loop(0, CH // STEP, make_hidden, 0)
    for d in (1, 2, 3):
        ag_copy(0, d).start()

    def partial_back(i, _):
        j = lax.rem(x + i + 1, 4)
        stg[0, i] = contract(gs[rows_of(j, CH)], wd[...], 1, 1)
        rs_copy(2, stg.at[0, i], i + 1).start()
        return 0

    lax.fori_loop(0, 3, partial_back, 0)
    own_b[...] = contract(gs[rows_of(x, CH)], wd[...], 1, 1)

    def p_copy(t, p, h):
        i = t * NP + p
        rr = rows_of(h, PART)
        return remote(ws[t].at[rr, rows_of(p, CH)], pr.at[i, rr], p_s.at[i, h], p_r.at[i, h], peer)

    def step_matrix(t, left, right):
        for s in range(2):
            load_b(t, s, s).start()
        lam = lam_l[t, 0:1, 0:1]

        def piece(p, _):
            cols = rows_of(p, CH)
            s = lax.rem(p, 2)
            gt[...] = contract(left[...], right[:, cols], 0, 0)
            load_b(t, p, s).wait()

            def inner(i, _):
                rr = rows_of(i, STEP_D)
                w, b = ws[t][rr, cols].astype(F32), cin[s, rr].astype(F32)
                g = gt[rr] * (1.0 / TOK)
                new_b = 0.9 * b + 0.1 * g
                new_w = w - 0.5 * (0.3 * g + 0.7 * new_b)
                ws[t][rr, cols] = jnp.where(lam > 0.5, new_w, new_b).astype(BF16)
                return 0

            def part(h, _):
                lax.fori_loop(h * (PART // STEP_D), (h + 1) * (PART // STEP_D), inner, 0)
                p_copy(t, p, h).start()
                return 0

            lax.fori_loop(0, PARTS, part, 0)

            @pl.when(p + 2 < NP)
            def _():
                load_b(t, p + 2, s).start()

            return 0

        lax.fori_loop(0, NP, piece, 0)

    ag_wait(0)
    step_matrix(0, hid, gs)

    for d in (1, 2, 3):
        rs_copy(2, stg.at[0, d - 1], d).wait()

    def make_grads(i, _):
        rr = rows_of(i, STEP)
        back = ((own_b[rr] + rcv[2, 0, rr]) + rcv[2, 1, rr]) + rcv[2, 2, rr]
        gate, up = stg[0, 3, rr], stg[1, 3, rr]
        sig = jax.nn.sigmoid(gate)
        wr = pl.ds(pl.multiple_of(x * CH + i * STEP, STEP), STEP)
        dgt[wr] = (back * up * sig * (1.0 + gate * (1.0 - sig))).astype(BF16)
        dup[wr] = (back * (gate * sig)).astype(BF16)
        return 0

    lax.fori_loop(0, CH // STEP, make_grads, 0)
    for t in (1, 2):
        for d in (1, 2, 3):
            ag_copy(t, d).start()

    def token_part(grads, w_ref, first):
        def step(j, _):
            part = jnp.dot(grads[rows_of(j, CH)], w_ref[...], preferred_element_type=F32)
            part = part.reshape(2, 2, BLK, D)
            two = rows_of(j, 2)
            if first:
                tp[two] = part
            else:
                tp[two] = tp[two] + part
            return 0

        lax.fori_loop(0, 4, step, 0)

    ag_wait(1)
    token_part(dgt, wg, True)
    step_matrix(1, dgt, xs)
    ag_wait(2)
    token_part(dup, wu, False)
    tc_copy = remote(tp.at[:, 1 - k], tc, tc_s.at[0], tc_s.at[1], sib)
    tc_copy.start()
    step_matrix(2, dup, xs)

    lam_copy.wait()

    def means(t, q_a, p_a, q_b, p_b):
        la = rebuild(lam_l[t, 0:1, 0:1])
        lb = rebuild(lam_r[t, 0:1, 0:1])
        q_a, p_a, q_b, p_b = (v.astype(F32) for v in (q_a, p_a, q_b, p_b))
        w = (la[0] * q_a + la[1] * p_a) + (lb[0] * q_b + lb[1] * p_b)
        b = (la[2] * q_a + la[3] * p_a) + (lb[2] * q_b + lb[3] * p_b)
        return (0.5 * w).astype(BF16), (0.5 * b).astype(BF16)

    def load_q(t, p, s):
        return pltpu.make_async_copy(qr.at[t * NP + p], cin.at[s], cin_s.at[s])

    def combine(t):
        for s in range(2):
            q_copy(t, s).wait()
            load_q(t, s, s).start()

        def piece(p, _):
            s = lax.rem(p, 2)
            i = t * NP + p
            cols = rows_of(p, CH)
            load_q(t, p, s).wait()

            def inner(n, _):
                rr = rows_of(n, STEP_D)
                w, b = means(t, qs[t][rr, cols], ws[t][rr, cols], cin[s, rr], pr[i, rr])
                ws[t][rr, cols] = w
                qs[t][rr, cols] = b
                return 0

            def part(h, _):
                p_copy(t, p, h).wait()
                return lax.fori_loop(h * (PART // STEP_D), (h + 1) * (PART // STEP_D), inner, 0)

            lax.fori_loop(0, PARTS, part, 0)

            @pl.when(p + 2 < NP)
            def _():
                q_copy(t, p + 2).wait()
                load_q(t, p + 2, s).start()

            return 0

        lax.fori_loop(0, NP, piece, 0)

    tc_copy.wait()

    def add_core(i, _):
        tc[i] = tc[i] + tp[i, k]
        return 0

    lax.fori_loop(0, 8, add_core, 0)

    def ty_copy(d, half):
        to = half * 4 + lax.rem(y + d, 4)
        return remote(tc.at[to], ty.at[d - 1, half], ty_s.at[d - 1, half], ty_r.at[d - 1, half], ydev[d])

    for d in (1, 2, 3):
        for half in range(2):
            ty_copy(d, half).start()

    combine(0)

    for d in (1, 2, 3):
        for half in range(2):
            ty_copy(d, half).wait()

    def along_y(half):
        return ((tc[half * 4 + y] + ty[0, half]) + ty[1, half]) + ty[2, half]

    tzs[...] = along_y(1 - zl).astype(BF16)
    tz_copy = remote(tzs, tz, tz_s.at[0], tz_s.at[1], zn)
    tz_copy.start()

    combine(1)

    mine = zl * 4 + y
    tc[mine] = along_y(zl)
    for m in range(2):
        for owner, n, dev in sends[m]:
            tok(m, owner, n, dev).wait_send()
    for t in range(3):
        for d in (1, 2, 3):
            ag_copy(t, d).wait_send()

    combine(2)

    tz_copy.wait()
    tgo[...] = (tc[mine] + tz[...].astype(F32)).astype(BF16)


def flush_kernel(*refs):
    n = len(refs) // 2
    copies = []
    for i in range(n):
        parts = 1 if refs[i].shape[0] < F else PARTS
        for h in range(parts):
            rr = pl.ds(h * (refs[i].shape[0] // parts), refs[i].shape[0] // parts)
            copies.append(pltpu.make_async_copy(refs[i].at[rr], refs[n + i].at[rr], refs[-1].at[i, h]))
    for cp in copies:
        cp.start()
    for cp in copies:
        cp.wait()


def flush(arrays):
    return pl.pallas_call(
        flush_kernel,
        out_shape=[jax.ShapeDtypeStruct(a.shape, a.dtype) for a in arrays],
        in_specs=[pl.BlockSpec(memory_space=pltpu.VMEM)] * len(arrays),
        out_specs=[pl.BlockSpec(memory_space=pl.ANY)] * len(arrays),
        scratch_shapes=[pltpu.SemaphoreType.DMA((len(arrays), PARTS))],
        compiler_params=pltpu.CompilerParams(vmem_limit_bytes=2**20),
    )(*[pltpu.with_memory_space_constraint(a, pltpu.VMEM) for a in arrays])


def body(tokens, grad_out, wg, wu, wd, bg, bu, bd):
    dma = pltpu.SemaphoreType.DMA
    whole = [(BLK, D)] + [(F, D)] * 6
    scratch = [
        pltpu.VMEM((TOK, D), BF16),
        pltpu.VMEM((TOK, D), BF16),
        pltpu.VMEM((3 * NP, F, CH), BF16),
        pltpu.VMEM((2, 4, CH, F), F32),
        pltpu.VMEM((CH, F), F32),
        pltpu.VMEM((3, 3, CH, F), F32),
        pltpu.VMEM((TOK, F), BF16),
        pltpu.VMEM((TOK, F), BF16),
        pltpu.VMEM((TOK, F), BF16),
        pltpu.VMEM((8, 2, BLK, D), F32),
        pltpu.VMEM((8, BLK, D), F32),
        pltpu.VMEM((3, 2, BLK, D), F32),
        pltpu.VMEM((BLK, D), BF16),
        pltpu.VMEM((BLK, D), BF16),
        pltpu.VMEM((F, CH), F32),
        pltpu.VMEM((2, F, CH), BF16),
        pltpu.VMEM((3, 8, 128), F32),
        pltpu.VMEM((3, 8, 128), F32),
        dma((5,)),
        dma((2,)),
        dma((2, 15)),
        dma((2, 16)),
        dma((3 * NP,)),
        dma((3 * NP,)),
        dma((3 * NP, PARTS)),
        dma((3 * NP, PARTS)),
        dma((2,)),
        dma((3, 3)),
        dma((3, 3)),
        dma((3, 3)),
        dma((3, 3)),
        dma((2,)),
        dma((3, 2)),
        dma((3, 2)),
        dma((2,)),
        dma((2,)),
    ]
    res = pl.pallas_call(
        kernel,
        out_shape=[pltpu.VMEM(s, BF16) for s in whole] + [jax.ShapeDtypeStruct((3 * NP, F, CH), BF16)],
        in_specs=[pl.BlockSpec(memory_space=pl.ANY)] * 8,
        out_specs=[pl.BlockSpec(memory_space=pltpu.VMEM)] * 7 + [pl.BlockSpec(memory_space=pl.ANY)],
        scratch_shapes=scratch,
        compiler_params=pltpu.CompilerParams(
            collective_id=0, has_side_effects=True, vmem_limit_bytes=48 * 2**20
        ),
        cost_estimate=pl.CostEstimate(
            flops=16 * TOK * D * F, bytes_accessed=40 * D * F, transcendentals=2 * CH * F
        ),
    )(tokens, grad_out, wg[0].T, wu[0].T, wd[0], bg[0].T, bu[0].T, bd[0])
    tg, gw, uw, dw, gb, ub, db = flush(res[:7])
    return tg, gw.T, uw.T, dw, gb.T, ub.T, db


def solution(mesh):
    weights = (P("rep", "row", "col"), P("rep", "row", "col"), P("rep", "col", "row"))
    means = (P("row", "col"), P("row", "col"), P("col", "row"))
    return jax.shard_map(
        body,
        mesh=mesh,
        in_specs=(P(("rep", "col"), "row"),) * 2 + weights * 2,
        out_specs=(P(("rep", "col"), "row"),) + means * 2,
        check_vma=False,
    )
```
